32 devices in a mesh: seq: 4 (over x, core), batch: 8 (over z, y).
Axes of the slice: x: 2, y: 2, z: 4, core: 2. Of those that a mesh axis runs over, the one named last changes fastest.
Arguments:
- inputs: bfloat16 [64, 512, 768], P('batch', 'seq'), may hold values from -6 to 6
- out_grad: float32 [64, 512, 768], P('batch', 'seq'), may hold values from -6 to 6
- out_mask: int32 [64, 512], P('batch', 'seq'), may hold values 0 or 1
- attn_mask: int32 [12, 512, 512], replicated, may hold values from 0 to 1, as said below
- mat_param: float32 [7077888], P(('seq', 'batch')), may hold values from -2 to 2
- mat_first: float32 [7077888], P(('seq', 'batch')), may hold values from -14 to 14
- mat_second: float32 [7077888], P(('seq', 'batch')), may hold values from 0.442368 to 1.769472
- vec_param: float32 [9216], P(('seq', 'batch')), may hold values from -1 to 2
- vec_first: float32 [9216], P(('seq', 'batch')), may hold values from -48 to 48
- vec_second: float32 [9216], P(('seq', 'batch')), may hold values from 4.9152 to 19.6608
Outputs:
- outputs: bfloat16 [64, 512, 768], P('batch', 'seq')
- input_grad: float32 [64, 512, 768], P('batch', 'seq')
- new_mats: float32 [7077888], P(('seq', 'batch'))
- new_mat_first: float32 [7077888], P(('seq', 'batch'))
- new_mat_second: float32 [7077888], P(('seq', 'batch'))
- new_vecs: float32 [9216], P(('seq', 'batch'))
- new_vec_first: float32 [9216], P(('seq', 'batch'))
- new_vec_second: float32 [9216], P(('seq', 'batch'))
The draws below stay inside these ranges and needn't reach their ends.
Inputs may be any that keep to these rules, and one draw needn't show every extreme that they name: `attn_mask`: every head's mask is 1 on its diagonal.
All inputs are finite; a program needn't handle non-finite values. No bound on the sum of `out_mask` on one device may be relied on, other than what follows from the above.
Results may differ from the reference program's by a relative error of at most 0.013.
Values may be sent and summed in bfloat16 or wider, within the bound.
A program may use at most 192 MiB of HBM per device.

```python
import math
import jax
import jax.numpy as jnp
from jax import lax

D = 768
H = 12
HD = 64
FF = 3072
L = 512
STEP = 10
SEQS = 64
TOKENS = 32768
MATS = 7077888
VECS = 9216
N_SEQ = 4


def draw_attn_mask(key, part):
    key = jax.random.fold_in(key, 11)
    block_key, cell_key = jax.random.split(key)
    span = L // N_SEQ
    blocks = jax.random.randint(block_key, (H, N_SEQ, N_SEQ), 0, 10) < 7
    blocks = blocks | jnp.eye(N_SEQ, dtype=bool)[None]
    block_full = jnp.repeat(jnp.repeat(blocks, span, 1), span, 2)
    cells = jax.random.randint(cell_key, (H, L, L), 0, 100) < 35
    diagonal = jnp.eye(L, dtype=bool)[None]
    return (block_full & cells | diagonal).astype(jnp.int32)


def draw_mat_param(key, part):
    key = jax.random.fold_in(key, 12)
    values = jax.random.truncated_normal(key, -4.0, 4.0, (MATS,), jnp.float32)
    index = jnp.arange(MATS)
    first = 3 * D * D
    second = first + D * D
    third = second + D * FF
    scales = jnp.where(index < first, D ** (-0.5), jnp.where(index < second, 4.0 * D ** (-0.5), jnp.where(index < third, D ** (-0.5), FF ** (-0.5))))
    return (values * scales).astype(jnp.float32)


def draw_vec_param(key, part):
    key = jax.random.fold_in(key, 13)
    normal_key, gain_key = jax.random.split(key)
    shifts = 0.2 * jax.random.truncated_normal(normal_key, -4.0, 4.0, (VECS,), jnp.float32)
    gains = jax.random.uniform(gain_key, (VECS,), jnp.float32, 0.7, 1.3)
    index = jnp.arange(VECS)
    gain_one = 4 * D + FF
    gain_two = 6 * D + FF
    is_gain = (index >= gain_one) & (index < gain_one + D) | (index >= gain_two) & (index < gain_two + D)
    return jnp.where(is_gain, gains, shifts).astype(jnp.float32)


def with_ends(array, stream_key, low, top_value):
    spot = [jax.random.randint(jax.random.fold_in(stream_key, axis), (), 0, length) for axis, length in enumerate(array.shape)]
    widest = array.shape.index(max(array.shape))
    beside = spot[:widest] + [(spot[widest] + 1) % array.shape[widest]] + spot[widest + 1:]
    return array.at[tuple(spot)].set(low).at[tuple(beside)].set(top_value)


def level_of(rng, dims, cuts, low, top_value):
    loudness = 1.0
    for dim, shards_of in cuts:
        draws = jax.random.uniform(jax.random.fold_in(jax.random.fold_in(rng, 6), dim), (shards_of,), jnp.float32, low / len(cuts), top_value / len(cuts))
        loudness = loudness * jnp.repeat(jnp.exp(draws), dims[dim] // shards_of).reshape((-1,) + (1,) * (len(dims) - 1 - dim))
    return loudness


def normal_values(own_key, dims, deviation, limit, cuts=(), held_as=jnp.bfloat16):
    entries = deviation * jax.random.normal(own_key, dims, jnp.float32)
    if cuts:
        entries = entries * level_of(own_key, dims, cuts, -0.22, 0.18)
    return jnp.clip(entries, -limit, limit).astype(held_as)


def setup_inputs(seed: int = 0) -> dict:
    arg_keys = jax.random.split(jax.random.key(seed), 11)
    return {
        "inputs": normal_values(arg_keys[0], (SEQS, L, D), 1.0, 6.0, ((0, 8), (1, 4))),
        "out_grad": normal_values(arg_keys[1], (SEQS, L, D), 1.0, 6.0, ((0, 8), (1, 4)), jnp.float32),
        "out_mask": with_ends((jax.random.randint(arg_keys[2], (SEQS, L), 0, 20) < 3).astype(jnp.int32), jax.random.fold_in(arg_keys[2], 1), 0, 1),
        "attn_mask": draw_attn_mask(jax.random.fold_in(arg_keys[10], 71), 0),
        "mat_param": draw_mat_param(jax.random.fold_in(arg_keys[10], 71), 0),
        "mat_first": normal_values(arg_keys[5], (MATS,), (0.033 * (0.15 * TOKENS) ** 0.5), 14.0, ((0, 32),), jnp.float32),
        "mat_second": jnp.clip(jnp.exp(math.log(1.769472) - 1.3862944 * jax.random.uniform(arg_keys[6], (MATS,), jnp.float32) ** level_of(arg_keys[6], (MATS,), ((0, 32),), -0.2, 0.2)), 0.442368, 1.769472),
        "vec_param": draw_vec_param(jax.random.fold_in(arg_keys[10], 71), 0),
        "vec_first": normal_values(arg_keys[8], (VECS,), (0.11 * (0.15 * TOKENS) ** 0.5), 48.0, ((0, 32),), jnp.float32),
        "vec_second": jnp.clip(jnp.exp(math.log(19.6608) - 1.3862944 * jax.random.uniform(arg_keys[9], (VECS,), jnp.float32) ** level_of(arg_keys[9], (VECS,), ((0, 32),), -0.2, 0.2)), 4.9152, 19.6608),
    }


@jax.custom_vjp
def low(v):
    return lax.optimization_barrier(v.astype(jnp.bfloat16)).astype(jnp.float32)

@jax.custom_vjp
def low_back(v):
    return v

def low_keep(v):
    return (low(v), None)

def low_pass(kept, grad):
    return (grad,)

def back_keep(v):
    return (v, None)

def back_low(kept, grad):
    return (low(grad),)
low.defvjp(low_keep, low_pass)
low_back.defvjp(back_keep, back_low)
NEG_FILL = -1e+30
NORM_EPS = 1e-06
ROOT_HALF = 0.7071067811865476
BETA_ONE = 0.9
BETA_TWO = 0.999
ADAM_EPS = 1e-08
DECAY_RATE = 0.01
MATS_RATE = 0.1
VECS_RATE = 0.5

def hdot(operand_one, operand_two):
    return jnp.dot(operand_one, operand_two, precision=lax.Precision.HIGHEST)

def layer_norm(values, gain, shift):
    center = values - lax.optimization_barrier(jnp.mean(values, -1, keepdims=True))
    spread = lax.optimization_barrier(jnp.mean(center * center, -1, keepdims=True))
    return center * lax.rsqrt(spread + NORM_EPS) * gain + shift

def gelu_exact(values):
    return 0.5 * values * (1.0 + lax.erf(values * ROOT_HALF))

def unpack_mats(flat):
    first = 3 * D * D
    second = first + D * D
    third = second + D * FF
    return (flat[:first].reshape(D, 3 * D), flat[first:second].reshape(D, D), flat[second:third].reshape(D, FF), flat[third:].reshape(FF, D))

def unpack_vecs(flat):
    pieces = []
    offset = 0
    for length in (D, D, D, FF, D, D, D, D, D):
        pieces.append(flat[offset:offset + length])
        offset = offset + length
    return pieces

def adam_step(param, first, second, grad, rate):
    first_new = BETA_ONE * first + (1.0 - BETA_ONE) * grad
    second_new = BETA_TWO * second + (1.0 - BETA_TWO) * grad * grad
    first_hat = first_new / (1.0 - BETA_ONE ** STEP)
    second_hat = second_new / (1.0 - BETA_TWO ** STEP)
    param_new = param - rate * (first_hat / (jnp.sqrt(second_hat) + ADAM_EPS) + DECAY_RATE * param)
    return (param_new, first_new, second_new)

def attend(queries, keys, values, keep):
    score_scale = 1.0 / math.sqrt(HD)
    raw = jnp.einsum('qhd,khd->hqk', queries, keys, precision=lax.Precision.HIGHEST) * score_scale
    scores = jnp.where(keep, low_back(raw), NEG_FILL)
    largest = lax.optimization_barrier(jnp.max(scores, -1, keepdims=True))
    expo = jnp.exp(scores - largest)
    probs = expo / lax.optimization_barrier(jnp.sum(expo, -1, keepdims=True))
    mixed = jnp.einsum('hqk,khd->qhd', low(probs), values, precision=lax.Precision.HIGHEST)
    return low(low_back(mixed)).reshape(L, D)

def forward(mats, vecs, block, keep):
    w_qkv, w_out, w_up, w_down = unpack_mats(low(mats))
    bias_query, bias_value, bias_out, bias_up, bias_down, gain_one, shift_one, gain_two, shift_two = unpack_vecs(low(vecs))
    seq_count = block.shape[0]
    flat_in = block.reshape(seq_count * L, D)
    proj = hdot(flat_in, w_qkv) + jnp.concatenate([bias_query, jnp.zeros_like(bias_query), bias_value])
    qkv = low(low_back(proj)).reshape(seq_count, L, 3, H, HD)

    def one_seq(triple):
        return attend(triple[0], triple[1], triple[2], keep)
    attended = lax.map(jax.checkpoint(one_seq), (qkv[:, :, 0], qkv[:, :, 1], qkv[:, :, 2]))
    attended = attended.reshape(seq_count * L, D)
    first_sum = flat_in + low_back(hdot(attended, w_out) + bias_out)
    hidden_one = layer_norm(first_sum, gain_one, shift_one)
    up_sum = low_back(hdot(low(hidden_one), w_up) + bias_up)
    act_low = low(gelu_exact(up_sum))
    second_sum = hidden_one + low_back(hdot(act_low, w_down) + bias_down)
    return layer_norm(second_sum, gain_two, shift_two)

def reference(inputs, out_grad, out_mask, attn_mask, mat_param, mat_first, mat_second, vec_param, vec_first, vec_second):
    keep = attn_mask > 0
    groups = SEQS // 8
    blocks_in = inputs.astype(jnp.float32).reshape(groups, 8, L, D)
    cotangents = (out_grad * out_mask[..., None].astype(jnp.float32)).reshape(groups, 8, L, D)

    def one_group(carry, pair):
        block, cotangent = pair
        result, pullback = jax.vjp(lambda mats, vecs, data: forward(mats, vecs, data, keep), mat_param, vec_param, block)
        grad_mats, grad_vecs, grad_data = pullback(cotangent.reshape(8 * L, D))
        return ((carry[0] + grad_mats, carry[1] + grad_vecs), (result.astype(jnp.bfloat16).reshape(8, L, D), grad_data))
    start = (jnp.zeros((MATS,), jnp.float32), jnp.zeros((VECS,), jnp.float32))
    (grad_mats, grad_vecs), (outputs, input_grad) = lax.scan(one_group, start, (blocks_in, cotangents))
    new_mats, new_mat_first, new_mat_second = adam_step(mat_param, mat_first, mat_second, grad_mats, MATS_RATE)
    new_vecs, new_vec_first, new_vec_second = adam_step(vec_param, vec_first, vec_second, grad_vecs, VECS_RATE)
    return (outputs.reshape(SEQS, L, D), input_grad.reshape(SEQS, L, D), new_mats, new_mat_first, new_mat_second, new_vecs, new_vec_first, new_vec_second)
```

```python
import functools
import math

import jax
import jax.numpy as jnp
from jax import lax
from jax.experimental import pallas as pl
from jax.experimental.pallas import tpu as pltpu
from jax.sharding import PartitionSpec as P

D = 768
FF = 3072
STEP = 10


NEG_FILL = -1e30
NORM_EPS = 1e-06
ROOT_HALF = 0.7071067811865476
ROOT_TWO_PI_INV = 0.3989422804014327
BETA_ONE = 0.9
BETA_TWO = 0.999
ADAM_EPS = 1e-08
DECAY_RATE = 0.01
MATS_RATE = 0.1
VECS_RATE = 0.5

BF16 = jnp.bfloat16
F32 = jnp.float32
MESH = pl.DeviceIdType.MESH
ANY = pl.BlockSpec(memory_space=pl.ANY)
VMEM = pl.BlockSpec(memory_space=pltpu.VMEM)
MIB = 1 << 20

MATRICES = (("qkv", 3 * D, 3), ("out", D, 1), ("up", FF, FF // D), ("down", FF, 1))
VEC_LENGTHS = (D, D, D, FF, D, D, D, D, D)


def layer_norm(values, gain, shift):
    center = values - jnp.mean(values, -1, keepdims=True)
    spread = jnp.mean(center * center, -1, keepdims=True)
    return center * lax.rsqrt(spread + NORM_EPS) * gain + shift


def gelu_exact(values):
    return 0.5 * values * (1.0 + lax.erf(values * ROOT_HALF))


def adam_step(param, first, second, grad, rate):
    first_new = BETA_ONE * first + (1.0 - BETA_ONE) * grad
    second_new = BETA_TWO * second + (1.0 - BETA_TWO) * grad * grad
    first_hat = first_new / (1.0 - BETA_ONE**STEP)
    second_hat = second_new / (1.0 - BETA_TWO**STEP)
    param_new = param - rate * (first_hat / (jnp.sqrt(second_hat) + ADAM_EPS) + DECAY_RATE * param)
    return (param_new, first_new, second_new)


def contract_rows(operand_one, operand_two):
    return lax.dot_general(
        operand_one, operand_two, (((0,), (0,)), ((), ())), preferred_element_type=jnp.float32
    )


def contract_cols(operand_one, operand_two):
    return lax.dot_general(
        operand_one, operand_two, (((1,), (1,)), ((), ())), preferred_element_type=jnp.float32
    )


def segments(share, rows):
    found, start = [], 0
    for name, length, pieces in MATRICES:
        low, high = max(start, share * rows), min(start + length, (share + 1) * rows)
        if low < high:
            found.append((name, pieces, low - share * rows, low - start, high - low))
        start += length
    return found


def by_columns(name, block, pieces):
    rows = block.shape[0]
    if name == "qkv":
        return block.reshape(rows // 3, 3, 3, D // 3).transpose(2, 0, 1, 3).reshape(rows, D)
    return block.reshape(rows // pieces, pieces, D).swapaxes(0, 1).reshape(rows, D)


def by_rows(name, block, pieces):
    rows = block.shape[0]
    if name == "qkv":
        return block.reshape(3, rows // 3, 3, D // 3).transpose(1, 2, 0, 3).reshape(rows, D)
    return block.reshape(pieces, rows // pieces, D).swapaxes(0, 1).reshape(rows, D)


def regroup(blocks):
    return blocks.reshape(3, D, 3, D // 3).transpose(2, 1, 0, 3).reshape(3, D, D)


def rearrange(share_index, shares, block, change):
    rows = block.shape[0]
    layouts, starts = [], []
    for share in range(shares):
        layout = tuple((name, pieces, at, size) for name, pieces, at, _, size in segments(share, rows))
        if not layouts or layout != layouts[-1]:
            layouts.append(layout)
            starts.append(share)

    def branch(layout, values):
        return jnp.concatenate([change(name, values[at : at + size], pieces) for name, pieces, at, size in layout])

    return lax.switch(
        sum((share_index >= start).astype(jnp.int32) for start in starts[1:]),
        [functools.partial(branch, layout) for layout in layouts],
        block,
    )


def take_matrix(gathered, name):
    shares, rows, _ = gathered.shape
    found = []
    for share in range(shares):
        for other, pieces, at, _, size in segments(share, rows):
            if other == name:
                found.append(gathered[share, at : at + size].reshape(pieces, size // pieces, D))
    return jnp.concatenate(found, 1)


def to_shares(blocks, shares):
    rows = sum(length for _, length, _ in MATRICES) // shares
    found = []
    for share in range(shares):
        for name, pieces, _, begin, size in segments(share, rows):
            part = blocks[name][:, begin // pieces : (begin + size) // pieces]
            found.append(part.reshape(size, D))
    return jnp.concatenate(found).reshape(shares, rows, D)


class Place:
    def __init__(self, n_batch):
        self.n_batch, self.n_z = n_batch, n_batch // 2
        self.seq, self.batch = lax.axis_index("seq"), lax.axis_index("batch")
        self.x, self.core = self.seq // 2, self.seq % 2
        self.z, self.y = self.batch // 2, self.batch % 2
        self.x_peer = {"seq": (1 - self.x) * 2 + self.core}
        self.core_peer = {"seq": self.x * 2 + 1 - self.core}
        self.y_peer = {"batch": self.z * 2 + 1 - self.y}
        self.ring = 2 * self.n_z
        self.position = (1 - self.y) * self.z + self.y * (self.ring - 1 - self.z)
        self.next, self.prev = {"batch": self.around(1)}, {"batch": self.around(-1)}

    def around(self, step):
        place = (self.position + step + self.ring) % self.ring
        y = place // self.n_z
        return 2 * ((1 - y) * place + y * (self.ring - 1 - place)) + y

    def share(self, x, core, step):
        return (2 * x + core) * self.n_batch + self.around(step)

    def z_at(self, step):
        return (self.z + step) % self.n_z

    def z_peer(self, step):
        return {"batch": self.z_at(step) * 2 + self.y}

    def seq_at(self, step):
        return (self.seq + step) % 4

    def seq_peer(self, step):
        return {"seq": self.seq_at(step)}

    def barrier(self):
        barrier = pltpu.get_barrier_semaphore()
        peers = [self.seq_peer(step) for step in (1, 2, 3)]
        peers += [self.y_peer] + [self.z_peer(step) for step in range(1, self.n_z)]
        for peer in peers:
            pl.semaphore_signal(barrier, inc=1, device_id=peer, device_id_type=MESH)
        pl.semaphore_wait(barrier, len(peers))


def run(steps):
    for step in steps:
        step()


def dispatch(now, steps, body):
    if len(steps) == 1:
        pl.when(now == steps[0])(functools.partial(body, steps[0]))
    elif steps:
        middle = len(steps) // 2
        lax.cond(
            now < steps[middle],
            lambda: dispatch(now, steps[:middle], body),
            lambda: dispatch(now, steps[middle:], body),
        )


class Sends:
    def __init__(self, sems):
        self.sems, self.started, self.when = sems, [], None

    def start(self, src, dst, recv_sem, peer, like=None):
        copy = pltpu.make_async_remote_copy(
            src_ref=src,
            dst_ref=dst,
            send_sem=self.sems.at[len(self.started)],
            recv_sem=recv_sem,
            device_id=peer,
            device_id_type=MESH,
        )
        copy.start()
        self.started.append((self.when, like or (lambda: src)))

    def arrived(self, dst, recv_sem, peer):
        pltpu.make_async_remote_copy(
            src_ref=dst,
            dst_ref=dst,
            send_sem=self.sems.at[0],
            recv_sem=recv_sem,
            device_id=peer,
            device_id_type=MESH,
        ).wait_recv()

    def sent(self, last, count, peer):
        for index in range(len(self.started) - last, len(self.started) - last + count):
            self.wait(index, self.started[index][1](), peer)
            self.started[index] = None

    def wait(self, index, ref, peer):
        pltpu.make_async_remote_copy(
            src_ref=ref,
            dst_ref=ref,
            send_sem=self.sems.at[index],
            recv_sem=self.sems.at[index],
            device_id=peer,
            device_id_type=MESH,
        ).wait_send()

    def under(self, condition, body):
        outer = self.when
        self.when = condition if outer is None else jnp.logical_and(outer, condition)

        @pl.when(condition)
        def _():
            body()

        self.when = outer

    def drain(self, peer):
        assert len(self.started) <= self.sems.shape[0]
        for index, (when, like) in [(i, one) for i, one in enumerate(self.started) if one]:
            if when is None:
                self.wait(index, like(), peer)
            else:
                pl.when(when)(lambda: self.wait(index, like(), peer))


def contract(one, two, dims):
    return lax.dot_general(one, two, ((dims[:1], dims[1:]), ((), ())), preferred_element_type=F32)


def half_of(shape, head):
    return lax.broadcasted_iota(jnp.int32, shape, 1) // 64 == head % 2


def row_of(grid, first, count):
    return jnp.concatenate([grid[first + i : first + i + 1, :] for i in range(count)], 1)


def attend_head(head, seq, qkv, mask, att, lse):
    lanes = pl.ds(pl.multiple_of(head // 2 * 128, 128), 128)
    length = mask.shape[0]
    block = 256
    k = qkv[1, seq, :, lanes]
    v = qkv[2, seq, :, lanes]
    v = jnp.where(half_of(v.shape, head), v, 1.0).astype(BF16)
    for i in range(length // block):
        rows = pl.ds(i * block, block)
        q = qkv[0, seq, rows, lanes]
        q = jnp.where(half_of(q.shape, head), q * 0.125, 0.0).astype(BF16)
        scores = contract(q, k, (1, 1))
        scores = jnp.where(mask[rows, :] > 0, scores, NEG_FILL)
        largest = jnp.max(scores, -1, keepdims=True)
        both = contract(jnp.exp(scores - largest).astype(BF16), v, (1, 0))
        turned = pltpu.roll(both, 64, 1)
        old = att[seq, rows, lanes]
        att[seq, rows, lanes] = jnp.where(half_of(old.shape, head), (both / turned).astype(BF16), old)
        total = jnp.where(head % 2 == 0, turned, both)
        kept = lse[seq, rows, :]
        lane = lax.broadcasted_iota(jnp.int32, kept.shape, 1)
        lse[seq, rows, :] = jnp.where(lane == head, largest + jnp.log(total), kept)


def head_backward(head, seq, qkv, mask, att, datt, lse, probs, dscore, dqkv):
    lanes = pl.ds(pl.multiple_of(head // 2 * 128, 128), 128)
    length = mask.shape[0]
    block = 256
    k = qkv[1, seq, :, lanes]
    v = qkv[2, seq, :, lanes]
    own = half_of(k.shape, head)
    k_own = jnp.where(own, k, 0.0).astype(BF16)
    for i in range(length // block):
        rows = pl.ds(i * block, block)
        q = qkv[0, seq, rows, lanes]
        g = datt[seq, rows, lanes]
        half = half_of(q.shape, head)
        q = jnp.where(half, q * 0.125, 0.0).astype(BF16)
        g = jnp.where(half, g, 0.0).astype(BF16)
        kept = lse[seq, rows, :]
        lane = lax.broadcasted_iota(jnp.int32, kept.shape, 1)
        total = jnp.sum(jnp.where(lane == head, kept, 0.0), -1, keepdims=True)
        inner = jnp.sum(g.astype(F32) * att[seq, rows, lanes].astype(F32), -1, keepdims=True)
        scores = contract(q, k, (1, 1))
        p = jnp.where(mask[rows, :] > 0, jnp.exp(scores - total), 0.0)
        d = p * (contract(g, v, (1, 1)) - inner)
        probs[rows, :] = p.astype(BF16)
        d = d.astype(BF16)
        dscore[rows, :] = d
        dq = contract(d, k_own, (1, 0)) * 0.125
        old = dqkv[0, seq, rows, lanes]
        dqkv[0, seq, rows, lanes] = jnp.where(half, dq.astype(BF16), old)
    q = qkv[0, seq, :, lanes]
    g = datt[seq, :, lanes]
    dk = contract(q.T, dscore[...], (1, 0)).T * 0.125
    dv = contract(g.T, probs[...], (1, 0)).T
    for j, value in ((1, dk), (2, dv)):
        old = dqkv[j, seq, :, lanes]
        dqkv[j, seq, :, lanes] = jnp.where(own, value.astype(BF16), old)


def add_rows(target, target_rows, *others):
    step = 32
    first, size = target_rows

    def body(i, carry):
        at = pl.ds(pl.multiple_of(first + i * step, 16), step)
        total = target[at].astype(F32)
        for ref, begin in others:
            total = total + ref[pl.ds(pl.multiple_of(begin + i * step, 16), step)].astype(F32)
        target[at] = total.astype(target.dtype)
        return carry

    lax.fori_loop(0, size // step, body, 0)


def norm_parts(values):
    center = values - jnp.mean(values, -1, keepdims=True)
    scale = lax.rsqrt(jnp.mean(center * center, -1, keepdims=True) + NORM_EPS)
    return center * scale, scale


def norm_back(grad, normed, scale, gain):
    dn = grad * gain
    along = jnp.mean(dn * normed, -1, keepdims=True)
    return (dn - jnp.mean(dn, -1, keepdims=True) - normed * along) * scale


BEFORE_UP, LAST_STEP = 72, 89
ACROSS_ORDER = (0, 1, -1, 2, -2, 3, -3, 4)
FIRST = {
    0: (("q", 1, 0), ("q_start", 1), ("q", 2, 0), ("q", 1, 1), ("q_start", 2), ("q", 3, 0), ("q", 2, 1), ("q", 1, 2), ("q", 4, 0)),
    2: (("q", 1, 0), ("q", 2, 0), ("q_start", 1), ("q", 3, 0), ("q", 1, 1), ("q", 4, 0)),
}
THEN = {
    0: (("q", 3, 1), ("q", 2, 2), ("q", 4, 1), ("q", 3, 2), ("q", 4, 2)),
    2: (("q", 2, 1), ("q_start", 2), ("q", 3, 1), ("q", 1, 2), ("q", 4, 1), ("q", 2, 2), ("q", 3, 2), ("q", 4, 2)),
}
TIMES = {
    0: dict(then=(0, 3, 4, 9, 89), far=(37, 49, 58, 66, 74), across=(0, 25, 30, 64, 80), dy=33),
    1: dict(own=(-1, 18, 24, 56, 64), over_x=0, far=(34, 43, 68, 76, 83), dy=27),
    2: dict(then=(0, 0, 0, 0, 11, 12, 17, 84), own=(1, 18, 27, 49, 57), over_x=0, dy=64),
    3: dict(own=(59, 69, 75, 83, 85), over_x=2, far=(3, 28, 43, 68, 76), across=(16, 23, 53, 56, 89), dy=21),
}


def timetable():
    found = []

    def put(seq, step, rank, limit, *what):
        found.append((min(step, limit), rank, len(found), seq, what))

    for seq, times in TIMES.items():
        put(seq, -1, 0, -1, "x", 1)
        group = 1
        for step, what in zip(times.get("then", ()), THEN.get(seq, ())):
            put(seq, step, 1, 12 * group - 1, *what)
            group += what == ("q", 4, 1)
        if seq % 2:
            for piece in (1, 2):
                put(seq, 12 * piece, 1, LAST_STEP, "q_from_core", piece)
        limit = LAST_STEP if seq == 3 else BEFORE_UP
        if "own" in times:
            for rank, (step, what) in enumerate(zip(times["own"], (("start",), *(("own", hops) for hops in range(1, 5))))):
                put(seq, step, 2 + (rank > 0), limit, *what)
            put(seq, times["over_x"], 2, limit, "over_x")
        limit = LAST_STEP if seq == 1 else BEFORE_UP
        if "far" in times:
            for rank, (step, what) in enumerate(zip(times["far"], (("far_start",), *(("far", hops) for hops in range(1, 5))))):
                put(seq, step, 4 + (rank > 0), limit, *what)
        if "across" in times:
            for i, place in enumerate(ACROSS_ORDER):
                step = max(times["across"][(i + 1) // 2], times["far"][abs(place)])
                put(seq, step, 6, BEFORE_UP, "across", place)
        put(seq, times["dy"], 7, LAST_STEP, "dy")
    table = {}
    for step, _, _, seq, what in sorted(found):
        table.setdefault((seq, step), []).append(what)
    return table


def forward_kernel(
    n_batch, plan, share, vec, x_in, grad_in, scored, mask,
    mats, x_out, qkv_out, att_out, lse_out, out_own, dr1_out, datt_out, act_out, du_out, h1_out, dz_out, da_out, sums,
    x_all, att, dy, dy_in, out, wide, datt, w_out, w_up, w_down, stage, act, act_t, slope, h1_t, dz, da, scales, biases, lse, masks, vecs, vec_in,
    own_sem, send_sem, mat_sem, vec_sem, seq_sem, w_sem, mask_sem, out_sem, load_sem, stage_sem, row_sem, give_sem, give_own, grad_sem,
):
    at = Place(n_batch)
    n_z, tokens = at.n_z, x_in.shape[1]
    half = at.ring // 2
    me = at.share(at.x, at.core, 0)
    sends = Sends(send_sem)
    heads = mask.shape[0]
    seqs, length = x_all.shape[:2]
    depth = share.shape[1]
    n_up = FF // D
    mine = pl.ds(at.seq * tokens, tokens)
    w, qkv = w_up, slope

    own = [
        pltpu.make_async_copy(share, mats.at[me], own_sem.at[0]),
        pltpu.make_async_copy(x_in.at[pl.ds(at.seq * seqs, seqs)], x_all.at[:, mine], own_sem.at[1]),
        pltpu.make_async_copy(dy_in.at[pl.ds(at.seq * seqs, seqs)], dy.at[:, mine], own_sem.at[2]),
    ]
    per_row = length // tokens
    grads = []
    for i in range(grad_in.shape[0]):
        there = wide.at[i // per_row, pl.ds(i % per_row * tokens, tokens)]
        grads.append(pltpu.make_async_copy(grad_in.at[i], there, grad_sem.at[i]))
    for copy in own[:2] + grads:
        copy.start()

    for unit in range(2):
        pltpu.make_async_copy(mask.at[unit], masks.at[unit], mask_sem.at[unit]).start()
    vecs[...] = vec[...]
    at.barrier()

    all_of = (0, 3, 0)
    first_of, rest_of = (0, 1, 0), (1, 3, 2)
    whole_ring = (all_of, ((0, 1, 0), (1, 3, 1)))
    rest_ring = (rest_of, ((1, 2, 1), (2, 3, 2)))

    def piece_ring(piece):
        part = (piece, piece + 1, piece)
        return (part, (part, None) if piece == 0 else (None, part))

    def part_at(index, part):
        return mats.at[index, pl.ds(part[0], part[1] - part[0])]

    def wait(index, part):
        sends.arrived(part_at(index, part), mat_sem.at[index, part[2]], at.core_peer)

    def pass_on(index, part, *peers):
        for peer in peers:
            sends.start(part_at(index, part), part_at(index, part), mat_sem.at[index, part[2]], peer, lambda: part_at(0, part))

    def lay_out(index, piece):
        rows = pl.ds(pl.multiple_of(index * depth, 32), depth)
        return pltpu.make_async_copy(mats.at[index, piece], w.at[piece, rows], w_sem.at[index, piece])

    def nothing(index):
        pass

    def round_start(x_at, ring):
        pass_on(at.share(x_at, at.core, 0), ring[0], at.next, at.prev)

    def round_step(x_at, hops, ring, then):
        for way, sign, peer in ((0, -1, at.next), (1, 1, at.prev)):
            index = at.share(x_at, at.core, sign * hops)
            part = ring[0] if hops < half else ring[1][way]
            if part:
                wait(index, part)
            onward = ring[0] if hops < half - 1 else ring[1][way] if hops == half - 1 else None
            if onward:
                pass_on(index, onward, peer)
            if hops < half:
                then(index)
        if hops == half:
            then(at.share(x_at, at.core, half))

    def vec_hop(hop, peer):
        vec_in[hop + n_z] = vecs[...]
        sends.start(vec_in.at[hop + n_z], vec_in.at[hop], vec_sem.at[hop], peer)

    def vec_take(hop):
        sends.arrived(vec_in.at[hop], vec_sem.at[hop], at.core_peer)
        vecs[...] = vecs[...] + vec_in[hop]

    def exchange(src, dst, which, seq):
        for step in (1, 2, 3):
            theirs = at.seq_at(step) * seqs + seq
            sends.start(src.at[theirs], dst.at[seq, mine], seq_sem.at[which, seq, step], at.seq_peer(step), lambda: src.at[0])

    def exchanged(dst, which, seq):
        for step in (1, 2, 3):
            theirs = pl.ds(at.seq_at(4 - step) * tokens, tokens)
            sends.arrived(dst.at[seq, theirs], seq_sem.at[which, seq, step], at.core_peer)

    is_class = [at.seq == seq for seq in range(4)]
    is_core0, is_core1 = at.core == 0, at.core == 1
    vec_hop(0, at.core_peer)
    own[0].wait()

    def q_arrived(piece, index):
        pass_on(index, piece_ring(piece)[0], at.core_peer)
        lay_out(index, piece).start()

    def q_start(seq, piece):
        index = at.share(0, 0, 0)
        if seq == 2:
            wait(index, piece_ring(piece)[0])
        round_start(0, piece_ring(piece))
        q_arrived(piece, index)

    def q_step(hops, piece):
        round_step(0, hops, piece_ring(piece), functools.partial(q_arrived, piece))

    def q_from_core(piece, first=0):
        for hops in range(first, half + 1):
            for sign in (-1, 1) if 0 < hops < half else (1,):
                index = at.share(0, 0, sign * hops)
                wait(index, piece_ring(piece)[0])
                lay_out(index, piece).start()

    def other_start(seq):
        round_start(at.x, whole_ring)
        pass_on(me, all_of, at.core_peer)

    def own_over_x(seq):
        if seq == 3:
            pass_on(me, all_of, at.x_peer)
        else:
            pass_on(me, rest_of, at.x_peer)
            pass_on(me, first_of, at.x_peer)

    def own_arrived(seq, index):
        if seq != 3:
            pass_on(index, first_of, at.x_peer)
        pass_on(index, all_of, at.core_peer)

    def far_arrived(index):
        pass_on(index, all_of, at.core_peer)

    def far_start(seq):
        index = at.share(1 - at.x, at.core, 0)
        ring = whole_ring if seq == 1 else rest_ring
        wait(index, ring[0])
        round_start(1 - at.x, ring)
        if seq == 1:
            far_arrived(index)

    def far_step(seq, hops):
        if seq == 1:
            round_step(1 - at.x, hops, whole_ring, far_arrived)
        else:
            round_step(1 - at.x, hops, rest_ring, nothing)

    def across(place):
        index = at.share(1 - at.x, at.core, place)
        wait(index, first_of)
        far_arrived(index)

    def relay(seq, what, *which):
        if what == "q":
            q_step(*which)
        elif what == "q_start":
            q_start(seq, *which)
        elif what == "q_from_core":
            q_from_core(*which)
        elif what == "start":
            other_start(seq)
        elif what == "over_x":
            own_over_x(seq)
        elif what == "own":
            round_step(at.x, *which, whole_ring, functools.partial(own_arrived, seq))
        elif what == "far_start":
            far_start(seq)
        elif what == "far":
            far_step(seq, *which)
        elif what == "across":
            across(*which)
        elif what == "x":
            exchange(x_in, x_all, 0, *which)
        else:
            for number in range(seqs):
                exchange(dy_in, dy, 1, number)

    def relay_all(seq, some):
        sends.under(is_class[seq], lambda: run([functools.partial(relay, seq, *one) for one in some]))

    def first_of_class0():
        pass_on(me, piece_ring(0)[0], at.x_peer)
        q_start(0, 0)
        sends.sent(4, 1, at.x_peer)
        exchange(x_in, x_all, 0, 0)
        for piece in (1, 2):
            pass_on(me, piece_ring(piece)[0], at.x_peer)

    def first_of_class1():
        index = at.share(0, 0, 0)
        wait(index, piece_ring(0)[0])
        lay_out(index, 0).start()
        exchange(x_in, x_all, 0, 0)

    def first_of_class2():
        exchange(x_in, x_all, 0, 0)
        q_start(2, 0)

    def first_of_class3():
        exchange(x_in, x_all, 0, 0)

    for seq, first in enumerate((first_of_class0, first_of_class1, first_of_class2, first_of_class3)):
        sends.under(is_class[seq], first)
    square = (tokens, tokens)
    diagonal = lax.broadcasted_iota(jnp.int32, square, 0) == lax.broadcasted_iota(jnp.int32, square, 1)
    for i, copy in enumerate(grads):
        copy.wait()
        column = jnp.sum(jnp.where(diagonal, scored[i : i + 1, :].astype(F32), 0.0), -1, keepdims=True)
        dy_in[i] = (wide[i // per_row, i % per_row * tokens : (i % per_row + 1) * tokens] * column).astype(BF16)
    own[2].start()
    vec_take(0)
    vec_hop(1, at.x_peer)
    for seq in (0, 2):
        relay_all(seq, FIRST[seq][:3])
    vec_take(1)
    vec_hop(2, at.y_peer)
    for seq in (0, 2):
        relay_all(seq, FIRST[seq][3:])
    sends.under(is_class[1], lambda: q_from_core(0, 1))
    sends.under(is_class[3], lambda: q_from_core(0))
    vec_take(2)
    vec_in[2 * n_z + 2] = vecs[...]
    for step in range(1, n_z):
        sends.start(vec_in.at[2 * n_z + 2], vec_in.at[2 + 2 * n_z + step], vec_sem.at[3 + step], at.z_peer(step))

    table = timetable()

    def relays(step):
        for seq in range(4):
            if (seq, step) in table:
                relay_all(seq, table[seq, step])

    def relays_in_loop(now, first, each, count):
        def turn(number):
            for step in range(first + number * each, first + (number + 1) * each):
                relays(step)

        held = {(step - first) // each for _, step in table if first <= step < first + each * count}
        dispatch(now, sorted(held), turn)

    relays(-1)
    for step in range(1, n_z):
        slot_in = 2 + 2 * n_z + step
        sends.arrived(vec_in.at[slot_in], vec_sem.at[3 + step], at.core_peer)
        vecs[...] = vecs[...] + vec_in[slot_in]
    exchanged(x_all, 0, 0)
    own[1].wait()

    grid = vecs[...]
    per = D // 128
    starts, offset = [], 0
    for size in VEC_LENGTHS:
        starts.append(offset // 128)
        offset += size
    width = D // 3
    b_q, b_v = row_of(grid, 0, per), row_of(grid, per, per)
    for piece in range(3):
        part = slice(piece * width, (piece + 1) * width)
        biases[piece, 0:1] = jnp.concatenate([b_q[:, part], jnp.zeros((1, width), F32), b_v[:, part]], 1)
    block = 256
    blocks = length // block
    outs = []

    def project(seq, piece):
        lanes = pl.ds(pl.multiple_of(piece * width, width), width)
        for i in range(blocks):
            rows = pl.ds(i * block, block)
            value = contract(x_all[seq, rows], w[piece], (1, 0)) + biases[piece, 0:1]
            for j in range(3):
                qkv[j, seq, rows, lanes] = value[:, j * width : (j + 1) * width].astype(BF16)

    lse[...] = jnp.zeros_like(lse)
    of_piece = heads // 3
    units = seqs * heads

    def fetch_mask(unit):
        slot = unit % 2
        return pltpu.make_async_copy(mask.at[unit % heads], masks.at[slot], mask_sem.at[slot])

    def one_head(unit, carry):
        seq, head = unit // heads, unit % heads
        relays_in_loop(unit, 0, 3, units)
        for piece in range(3):

            @pl.when(unit == piece * of_piece)
            def _():
                for index in range(2 * n_z):
                    lay_out(index, piece).wait()

        @pl.when(unit == heads)
        def _():
            exchanged(x_all, 0, 1)

        @pl.when(unit % of_piece == 0)
        def _():
            project(seq, head // of_piece)

        fetch_mask(unit).wait()

        attend_head(head, seq, qkv, masks.at[unit % 2], att, lse)

        @pl.when(unit + 2 < units)
        def _():
            fetch_mask(unit + 2).start()

        return carry

    lax.fori_loop(0, units, one_head, 0)
    outs.append(pltpu.make_async_copy(x_all, x_out, out_sem.at[0]))
    outs.append(pltpu.make_async_copy(qkv.at[pl.ds(0, 3)], qkv_out, out_sem.at[1]))
    outs.append(pltpu.make_async_copy(att, att_out, out_sem.at[2]))
    outs.append(pltpu.make_async_copy(lse, lse_out, out_sem.at[3]))
    for copy in outs:
        copy.start()
    relays(BEFORE_UP)

    def plane_from_core(x_at):
        for step in range(at.ring):
            wait(at.share(x_at, 1 - at.core, step), all_of)

    plane_from_core(at.core)
    loads = {"out": [], "down": []}
    for number, (name, share_at, first, begin, size) in enumerate(plan):
        if name != "up":
            target = {"out": w_out, "down": w_down}[name]
            source = mats.at[share_at, pl.ds(first // depth, size // depth)]
            loads[name].append(pltpu.make_async_copy(source, target.at[pl.ds(begin // depth, size // depth)], load_sem.at[number]))
    for copy in loads["out"]:
        copy.start()
    ups = [entry for entry in plan if entry[0] == "up"]
    pairs, group, filled = [], [], 0
    for _, share_at, first, _, size in ups:
        group.append((share_at, first, size))
        filled += size
        if filled // n_up % 16 == 0:
            pairs.append(group)
            group, filled = [], 0

    def fetch(number):
        slot = number % 2
        return [
            pltpu.make_async_copy(
                mats.at[share_at, pl.ds(first // depth, size // depth)],
                stage.at[slot, i, pl.ds(0, size // depth)],
                stage_sem.at[slot, i],
            )
            for i, (share_at, first, size) in enumerate(pairs[number])
        ]

    outs[1].wait()
    for copy in fetch(0):
        copy.start()
    line = 0
    for number, members in enumerate(pairs):
        if number + 1 < len(pairs):
            for copy in fetch(number + 1):
                copy.start()
        for copy in fetch(number):
            copy.wait()
        lines = sum(size for _, _, size in members) // n_up
        for j in range(n_up):
            pieces = []
            for i, (_, _, size) in enumerate(members):
                each = size // n_up
                low, high = j * each // 16 * 16, -(-(j + 1) * each // 16) * 16
                values = stage[number % 2, i].reshape(3 * depth, D)[low:high].astype(F32)
                pieces.append(values[j * each - low : j * each - low + each])
            w_up[j, line : line + lines] = jnp.concatenate(pieces, 0).astype(BF16)
        line += lines
    for copy in loads["out"]:
        copy.wait()

    b_o, b_2, g_1, s_1, g_2, s_2 = (row_of(grid, starts[i], per) for i in (2, 4, 5, 6, 7, 8))
    n_chunks = seqs * blocks

    def columns(i):
        return pl.ds(pl.multiple_of(i * block, block), block)

    def up_chunk(i, carry):
        relays_in_loop(i, BEFORE_UP + 1, n_up, n_chunks)
        seq, rows = i // blocks, columns(i % blocks)
        mixed = contract(att[seq, rows], w_out[...].reshape(D, D), (1, 0))
        n1, scale1 = norm_parts(x_all[seq, rows].astype(F32) + mixed + b_o)
        wide[seq, rows] = n1
        scales[seq, rows] = jnp.broadcast_to(scale1, (block, 128))
        h1_low = (n1 * g_1 + s_1).astype(BF16)
        h1_t[:, columns(i)] = h1_low.T
        for j in range(n_up):
            value = contract(h1_low, w_up[j], (1, 0)) + row_of(grid, starts[3] + j * per, per)
            phi = 0.5 * (1.0 + lax.erf(value * ROOT_HALF))
            act[j, seq, rows] = (value * phi).astype(BF16)
            slope[j, seq, rows] = (phi + value * (jnp.exp(-0.5 * value * value) * ROOT_TWO_PI_INV)).astype(BF16)
        return carry

    lax.fori_loop(0, n_chunks, up_chunk, 0)
    outs.append(pltpu.make_async_copy(h1_t, h1_out, out_sem.at[4]))
    outs[4].start()
    relays(LAST_STEP)

    sends.under(is_core0, functools.partial(plane_from_core, 1))
    for copy in loads["down"]:
        copy.start()
    for seq in range(seqs):
        exchanged(dy, 1, seq)
    own[2].wait()
    sums[...] = jnp.zeros_like(sums)
    for copy in loads["down"]:
        copy.wait()

    def rows_out(i):
        seq, rows = i // blocks, columns(i % blocks)
        pairs_of = (
            (wide.at[seq, rows], dr1_out.at[seq, rows]),
            (datt.at[seq, rows], datt_out.at[seq, rows]),
            (act_t.at[:, columns(i)], act_out.at[:, columns(i)]),
            (slope.at[:, seq, rows], du_out.at[:, seq, rows]),
            (dz.at[seq, rows], dz_out.at[seq, rows]),
            (da.at[seq, rows], da_out.at[seq, rows]),
        )
        return [pltpu.make_async_copy(src, dst, row_sem.at[k, i]) for k, (src, dst) in enumerate(pairs_of)]

    holders = block // tokens

    def give(i, e):
        seq = i // blocks
        holder = i % blocks * holders + e
        src = out.at[seq, pl.ds(pl.multiple_of(holder * tokens, tokens), tokens)]
        dst = out_own.at[at.seq * seqs + seq]
        step = (holder - at.seq + 4) % 4
        remote = pltpu.make_async_remote_copy(
            src_ref=src,
            dst_ref=dst,
            send_sem=give_sem.at[0, i, e],
            recv_sem=give_sem.at[1, seq, step],
            device_id={"seq": holder},
            device_id_type=MESH,
        )
        return holder != at.seq, remote, pltpu.make_async_copy(src, dst, give_own.at[seq])

    def down_chunk(i, carry):
        seq, rows = i // blocks, columns(i % blocks)
        n1 = wide[seq, rows]
        scale1 = scales[seq, rows][:, 0:1]
        total = n1 * g_1 + s_1 + b_2
        for j in range(n_up):
            value = act[j, seq, rows]
            act_t[pl.ds(j * D, D), columns(i)] = value.T
            total = total + contract(value, w_down[pl.ds(j * D // depth, D // depth)].reshape(D, D), (1, 0))
        n2, scale2 = norm_parts(total)
        out[seq, rows] = (n2 * g_2 + s_2).astype(BF16)
        for e in range(holders):
            away, remote, here = give(i, e)
            pl.when(away)(remote.start)
            pl.when(jnp.logical_not(away))(here.start)
        d = dy[seq, rows].astype(F32)
        sums[0:1] += jnp.sum(d * n2, 0, keepdims=True)
        sums[1:2] += jnp.sum(d, 0, keepdims=True)
        dr2 = norm_back(d, n2, scale2, g_2)
        dz_low = dr2.astype(BF16)
        dz[seq, rows] = dz_low
        dh1 = dr2
        for j in range(n_up):
            grad = contract(dz_low, w_down[pl.ds(j * D // depth, D // depth)].reshape(D, D), (1, 1))
            du = (grad * slope[j, seq, rows].astype(F32)).astype(BF16)
            slope[j, seq, rows] = du
            dh1 = dh1 + contract(du, w_up[j], (1, 1))
        sums[2:3] += jnp.sum(dh1 * n1, 0, keepdims=True)
        sums[3:4] += jnp.sum(dh1, 0, keepdims=True)
        d1 = norm_back(dh1, n1, scale1, g_1)
        wide[seq, rows] = d1
        da_low = d1.astype(BF16)
        da[seq, rows] = da_low
        datt[seq, rows] = contract(da_low, w_out[...].reshape(D, D), (1, 1)).astype(BF16)
        for copy in rows_out(i):
            copy.start()
        return carry

    lax.fori_loop(0, n_chunks, down_chunk, 0)

    for i in range(n_chunks):
        for copy in rows_out(i):
            copy.wait()
        for e in range(holders):
            away, remote, here = give(i, e)
            pl.when(away)(remote.wait_send)
            pl.when(jnp.logical_not(away))(here.wait)
    for seq in range(seqs):
        for step in (1, 2, 3):
            dst = out_own.at[at.seq_at(4 - step) * seqs + seq]
            sends.arrived(dst, give_sem.at[1, seq, step], at.core_peer)
    for copy in outs[:1] + outs[2:]:
        copy.wait()
    sends.drain(at.core_peer)


def forward(n_batch, share, vec, x_in, grad_in, scored, mask):
    rows = share.shape[0]
    depth = rows // 3
    shares = 4 * n_batch
    n_z = n_batch // 2
    n_up = FF // D
    seqs, length = x_in.shape[0] // 4, 4 * x_in.shape[1]
    tokens = seqs * length
    plan = []
    for number in range(shares):
        for name, _, at, begin, size in segments(number, rows):
            if name != "qkv":
                plan.append((name, number, at, begin, size))
    whole, low, gelu = (seqs, length, D), (D, tokens), (n_up, seqs, length, D)
    share = share.reshape(3, depth, D)
    outs = [
        ((shares,) + share.shape, BF16),
        (whole, BF16),
        ((3,) + whole, BF16),
        (whole, BF16),
        ((seqs, length, 128), F32),
        (x_in.shape, BF16),
        (whole, F32),
        (whole, BF16),
        ((FF, tokens), BF16),
        (gelu, BF16),
        (low, BF16),
        (whole, BF16),
        (whole, BF16),
        ((8, D), F32),
    ]
    vmem = [
        (whole, BF16),
        (whole, BF16),
        (whole, BF16),
        (x_in.shape, BF16),
        (whole, BF16),
        (whole, F32),
        (whole, BF16),
        ((D // depth, depth, D), BF16),
        ((n_up, D, D), BF16),
        ((FF // depth, depth, D), BF16),
        ((2, 2, 3, depth, D), BF16),
        (gelu, BF16),
        ((FF, tokens), BF16),
        (gelu, BF16),
        (low, BF16),
        (whole, BF16),
        (whole, BF16),
        ((seqs, length, 128), F32),
        ((3, 8, D), F32),
        ((seqs, length, 128), F32),
        ((2, length, length), jnp.int32),
        (vec.shape, F32),
        ((3 * n_z + 3,) + vec.shape, F32),
    ]
    blocks = tokens // 256
    sems = [(3,), (400,), (shares, 3), (n_z + 3,), (2, seqs, 4), (2 * n_z, 3), (2,), (5,), (len(plan),), (2, 2), (6, blocks), (2, blocks, 4), (seqs,), (x_in.shape[0],)]
    return pl.pallas_call(
        functools.partial(forward_kernel, n_batch, plan),
        out_shape=[jax.ShapeDtypeStruct(shape, dtype) for shape, dtype in outs],
        in_specs=[ANY, VMEM, ANY, ANY, VMEM, ANY],
        out_specs=[ANY] * 13 + [VMEM],
        scratch_shapes=[pltpu.VMEM(shape, dtype) for shape, dtype in vmem]
        + [pltpu.SemaphoreType.DMA(shape) for shape in sems],
        compiler_params=pltpu.CompilerParams(
            collective_id=0, has_side_effects=True, vmem_limit_bytes=60 * MIB
        ),
        name="forward",
    )(share, vec, x_in, grad_in, scored, mask)


PLACES = (4, 3, -3, 2, -2, 1, -1, 0)
REDUCE_TIMES = {
    0: dict(over_x=(-2, -2, 0, 14, 8, 13, 8, 17), late=((5, 13, 16, 26, 28, 28), (16, 19, 22, 24, 28, 28), (3, 3, 5, 27, 28, 28))),
    1: dict(kind0=(9, 20, 27, 28, 28), kind1=(0, 5, 9, 15, 17, 22)),
    2: dict(kind0=(5, 9, 25, 27, 28), late=((12, 14, 16, 17, 21, 28), (16, 18, 21, 24, 25, 25), (16, 16, 25, 26, 27, 28))),
    3: dict(over_x=(4, 7, 7, 17, 9, 12, 11, 17), kind1=(0, 6, 10, 19, 27, 27)),
}


def reduction_table():
    found = []
    ring = (("begin",), ("hop", 1), ("hop", 2), ("hop", 3), ("end",), ("last",))
    for seq, times in REDUCE_TIMES.items():
        for i, step in enumerate(times.get("over_x", ())):
            found.append((step, 0, i, seq, ("x", PLACES[i])))
        for kind in (0, 1):
            for i, step in enumerate(times.get(f"kind{kind}", ())):
                found.append((step, 1 + kind, i, seq, ("ring", kind, None) + ring[i]))
        for piece in range(3):
            for i, step in enumerate(times.get("late", ((), (), ()))[piece]):
                found.append((max(step, 8 * (piece + 1)), 3 + piece, i, seq, ("ring", 1, piece) + ring[i]))
    table = {}
    for step, _, _, seq, what in sorted(found):
        table.setdefault((seq, step), []).append(what)
    return table


def finish_kernel(
    n_batch, mask, qkv_in, att_in, datt_in, lse_in, x_in, mats, dr1_in, act_in, du_in, h1_in, dz_in, da_in, sums,
    share, vec_out, dx_own,
    qkv, att, datt, lse, w, wide, dqkv, dx, turned, act_t, masks, probs, dscore, grads, from_core, x_a, ring_in, x_b, vec_in,
    in_sem, mask_sem, act_sem, du_sem, own_sem, send_sem, core_sem, a_sem, ring_sem, b_sem, vec_sem, seq_sem,
):
    at = Place(n_batch)
    rows = grads.shape[2]
    heads = mask.shape[0]
    n_z, tokens = at.n_z, dx_own.shape[1]
    seqs, length = att.shape[:2]
    depth = rows // 3
    n_up = FF // D
    half = at.ring // 2
    sends = Sends(send_sem)
    mine = pl.ds(at.seq * tokens, tokens)
    dz, da, x = dqkv.at[2], dx, dx

    ins = [
        pltpu.make_async_copy(src, dst, in_sem.at[i])
        for i, (src, dst) in enumerate(
            ((dz_in, dz), (att_in, att), (h1_in, turned), (da_in, da), (qkv_in, qkv), (datt_in, datt), (lse_in, lse))
        )
    ]

    def fetch_act(j):
        return pltpu.make_async_copy(act_in.at[pl.ds(j * D, D)], act_t.at[j % 2], act_sem.at[j % 2])

    def fetch_du(j):
        return pltpu.make_async_copy(du_in.at[j], dqkv.at[j % 2], du_sem.at[j % 2])

    def fetch_mask(head):
        slot = head % 2
        return pltpu.make_async_copy(mask.at[head], masks.at[slot], mask_sem.at[slot])

    ins[0].start()
    down_order = [*range(1, n_up), 0]
    fetch_act(down_order[0]).start()
    fetch_act(down_order[1]).start()
    for copy in ins[1:]:
        copy.start()
    fetch_du(0).start()
    fetch_du(1).start()
    fetch_mask(0).start()
    fetch_mask(1).start()
    loads = []
    for index in range(n_batch):
        target = w.at[:, pl.ds(index * depth, depth)]
        loads.append(pltpu.make_async_copy(mats.at[index], target, in_sem.at[9 + index]))
        loads[-1].start()
    at.barrier()

    is_class = [at.seq == seq for seq in range(4)]
    on_core = (at.core == 0, at.core == 1)

    def plane_of(core, kind):
        return (2 - core, 3 * core)[kind]

    order = [half] + [sign * hops for hops in range(half - 1, 0, -1) for sign in (1, -1)] + [0]

    def part_rows(part):
        return pl.ds(part[0] * depth, (part[1] - part[0]) * depth)

    def to_core(core, kind, part=(0, 3)):
        lines = part_rows(part)
        for step in order:
            b = at.around(step)
            source = grads.at[plane_of(1 - core, kind), b, lines]
            sends.start(source, from_core.at[kind, b, lines], core_sem.at[kind, b, part[0]], at.core_peer, lambda: from_core.at[0, 0, lines])

    def is_own(seq, kind):
        return (seq // 2 == seq % 2) == (kind == 1)

    def ring_of(own, kind, piece):
        if piece is not None:
            part = (piece, piece + 1)
            return part, (part, None) if piece == 0 else (None, part)
        if kind == 1 or own:
            return (0, 3), ((0, 1), (1, 3))
        return None, (None, None)

    def add(seq, kind, b, part, *others, into=None):
        low, high = part
        terms = [grads.at[plane_of(seq % 2, kind), b], *others]
        if kind == 0 and is_own(seq, 0):
            terms.append(x_a.at[b])
        lines = part_rows(part)
        target = from_core.at[kind, b]
        if into is not None:
            into[lines] = from_core[kind, b, lines].astype(F32)
            target = into
        add_rows(target, (low * depth, (high - low) * depth), *[(ref, low * depth) for ref in terms])

    def ready(seq, kind, b, piece):
        part = (0, 3) if piece is None else (piece, piece + 1)
        here = from_core.at[kind, b, part_rows(part)]
        if not (kind == 0 and not is_own(seq, 0)):
            sends.arrived(here, core_sem.at[kind, b, part[0]], at.core_peer)
        if kind == 0 and is_own(seq, 0):
            sends.arrived(x_a.at[b], a_sem.at[b], at.core_peer)

    def ring_send(kind, b, way, hops, part):
        peer = (at.next, at.prev)[way]
        lines = part_rows(part)
        sends.start(from_core.at[kind, b, lines], ring_in.at[kind, way, hops, lines], ring_sem.at[kind, way, hops, part[0]], peer, lambda: ring_in.at[0, 0, 0, lines])

    def ring_wait(kind, way, hops, part):
        sends.arrived(ring_in.at[kind, way, hops, part_rows(part)], ring_sem.at[kind, way, hops, part[0]], at.core_peer)
        return ring_in.at[kind, way, hops]

    def ring_step(seq, kind, piece, what, hops=0):
        own = is_own(seq, kind)
        whole, opposite = ring_of(own, kind, piece)
        if what == "begin":
            b = at.around(half)
            ready(seq, kind, b, piece)
            for way, part in enumerate(opposite):
                if part:
                    add(seq, kind, b, part)
                    ring_send(kind, b, way, 0, part)
        elif what == "hop":
            for way, b in enumerate((at.around(half - hops), at.around(hops - half))):
                ready(seq, kind, b, piece)
                if hops > 1:
                    add(seq, kind, b, whole, ring_wait(kind, way, hops - 1, whole))
                else:
                    part = opposite[way]
                    if part:
                        add(seq, kind, b, part, ring_wait(kind, way, 0, part))
                    for low, high in ((whole[0], part[0]), (part[1], whole[1])) if part else (whole,):
                        if low < high:
                            add(seq, kind, b, (low, high))
                ring_send(kind, b, way, hops, whole)
        elif what == "end":
            b = at.batch
            ready(seq, kind, b, piece)
            others = [ring_wait(kind, way, half - 1, whole) for way in range(2)]
            add(seq, kind, b, whole, *others, into=share if own else None)
            if not own:
                lines = part_rows(whole)
                sends.start(from_core.at[kind, b, lines], x_b.at[lines], b_sem.at[whole[0]], at.x_peer, lambda: x_b.at[lines])
        elif own:
            far_part = ring_of(False, kind, piece)[0]
            sends.arrived(x_b.at[part_rows(far_part)], b_sem.at[far_part[0]], at.core_peer)
            add_rows(share, (far_part[0] * depth, (far_part[1] - far_part[0]) * depth), (x_b, far_part[0] * depth))

    def over_x(seq, step):
        b = at.around(step)
        here = from_core.at[0, b]
        sends.arrived(here, core_sem.at[0, b, 0], at.core_peer)
        add(seq, 0, b, (0, 3))
        sends.start(here, x_a.at[b], a_sem.at[b], at.x_peer, lambda: x_a.at[0])

    table = reduction_table()

    def reduce_at(step):
        for seq in range(4):
            some = table.get((seq, step))
            if some:
                steps = [functools.partial(over_x if what[0] == "x" else ring_step, seq, *what[1:]) for what in some]
                sends.under(is_class[seq], functools.partial(run, steps))

    base_down, base_up, base_out = 3 * D + D + FF, 3 * D + D, 3 * D

    def put(row, values):
        done = 0
        while done < values.shape[0]:
            number, first = (row + done) // rows, (row + done) % rows
            size = min(values.shape[0] - done, rows - first)
            grads[number // n_batch, number % n_batch, first : first + size] = values[done : done + size]
            done += size

    starts, offset = [], 0
    for size in VEC_LENGTHS:
        starts.append(offset // 128)
        offset += size
    per = D // 128

    def put_vec(first, value):
        for i in range(value.shape[1] // 128):
            vec_out[first + i : first + i + 1, :] = value[0:1, i * 128 : (i + 1) * 128]

    ones = jnp.ones((16, seqs * length), BF16)
    block = D // 2

    def flat(values):
        return values.reshape(seqs * length, D)

    vec_out[...] = jnp.zeros_like(vec_out)
    ins[0].wait()
    for number, j in enumerate(down_order):
        fetch_act(j).wait()
        for i in range(D // block):
            put(base_down + j * D + i * block, contract(act_t[j % 2, i * block : (i + 1) * block], flat(dz[...]), (1, 0)).astype(BF16))
        if number + 2 < n_up:
            fetch_act(down_order[number + 2]).start()
        if number == n_up - 2:
            sends.under(on_core[0], functools.partial(to_core, 0, 1))
    put_vec(starts[4], contract(ones, flat(dz[...]), (1, 0)))
    reduce_at(-3)
    ins[2].wait()
    ups = []
    for number in range(4 * n_batch):
        ups += [(number, at_row, begin, size) for name, _, at_row, begin, size in segments(number, rows) if name == "up"]
    middle = D // 2
    for high in (1, 0):
        for pair in range(n_up // 2):
            for k in range(2):
                j = pair * 2 + k
                fetch_du(j).wait()
                wide[k, 0:middle] = contract(turned[high * middle : (high + 1) * middle], flat(dqkv[j % 2]), (1, 0))
                if high:
                    put_vec(starts[3] + j * per, contract(ones, flat(dqkv[j % 2]), (1, 0)))
                if not (high == 0 and pair == n_up // 2 - 1):
                    fetch_du((j + 2) % n_up).start()
            for number, at_row, begin, size in ups:
                count, low = size // n_up, begin // n_up - high * middle
                if 0 <= low < middle:
                    both = jnp.concatenate([wide[k, low : low + count] for k in range(2)], 0).astype(BF16)
                    at_row += pair * 2 * count
                    grads[number // n_batch, number % n_batch, at_row : at_row + 2 * count] = both
        if high:
            sends.under(on_core[1], functools.partial(to_core, 1, 0))
            reduce_at(-2)
    ins[1].wait()
    ins[3].wait()
    for seq in range(seqs):
        turned[:, seq * length : (seq + 1) * length] = att[seq].T
    for i in range(D // block):
        put(base_out + i * block, contract(turned[i * block : (i + 1) * block], flat(da[...]), (1, 0)).astype(BF16))
    sends.under(on_core[0], functools.partial(to_core, 0, 0))
    put_vec(starts[2], contract(ones, flat(da[...]), (1, 0)))
    for i, line in enumerate((starts[7], starts[8], starts[5], starts[6])):
        put_vec(line, sums[i : i + 1])

    dr1_copy = pltpu.make_async_copy(dr1_in, wide, in_sem.at[8])
    dr1_copy.start()
    x_copy = pltpu.make_async_copy(x_in, x, in_sem.at[7])
    x_copy.start()
    for copy in ins[4:]:
        copy.wait()
    x_copy.wait()
    for seq in range(seqs):
        turned[:, seq * length : (seq + 1) * length] = x[seq].T

    reduce_at(-1)

    units = heads * seqs
    of_piece = heads // 3
    width = D // 3
    lines = 4 * depth

    def qkv_gradient(piece):
        lanes = slice(piece * width, (piece + 1) * width)
        for j in range(3):
            right = dqkv[j, :, :, lanes].reshape(seqs * length, width)
            for i in range(D // lines):
                total = contract(turned[i * lines : (i + 1) * lines], right, (1, 0)).astype(BF16)
                for k in range(4):
                    grads[0, 4 * i + k, piece * depth : (piece + 1) * depth, j * width : (j + 1) * width] = total[k * depth : (k + 1) * depth]
        sends.under(on_core[1], functools.partial(to_core, 1, 1, (piece, piece + 1)))

    def one_head(head, carry):
        fetch_mask(head).wait()

        def one_seq(seq, carry):
            dispatch(head * seqs + seq, [step for step in range(units) if any((some, step) in table for some in range(4))], reduce_at)
            head_backward(head, seq, qkv, masks.at[head % 2], att, datt, lse, probs, dscore, dqkv)
            return carry

        lax.fori_loop(0, seqs, one_seq, 0)

        @pl.when(head + 2 < heads)
        def _():
            fetch_mask(head + 2).start()

        for piece in range(3):
            pl.when(head == (piece + 1) * of_piece - 1)(functools.partial(qkv_gradient, piece))
        return carry

    lax.fori_loop(0, heads, one_head, 0)
    for j in (0, 2):
        put_vec(starts[j // 2], contract(ones, flat(dqkv[j]), (1, 0)))

    def vec_hop(hop, peer):
        vec_in[hop + n_z] = vec_out[...]
        sends.start(vec_in.at[hop + n_z], vec_in.at[hop], vec_sem.at[hop], peer)

    def vec_take(hop):
        sends.arrived(vec_in.at[hop], vec_sem.at[hop], at.core_peer)
        vec_out[...] = vec_out[...] + vec_in[hop]

    vec_hop(0, at.core_peer)

    dr1_copy.wait()
    for copy in loads:
        copy.wait()
    for number, step in enumerate((1, 2, 3, 0)):
        reduce_at(units + number)
        theirs = pl.ds(pl.multiple_of(at.seq_at(step) * tokens, tokens), tokens)
        for seq in range(seqs):
            total = wide[seq, theirs]
            for j in range(3):
                for piece in range(3):
                    left = dqkv[j, seq, theirs, piece * width : (piece + 1) * width]
                    total = total + contract(left, w[piece, :, j * width : (j + 1) * width], (1, 1))
            dx[seq, theirs] = total.astype(BF16)
        there = dx_own.at[pl.ds(at.seq * seqs, seqs)]
        if step:
            sends.start(dx.at[:, theirs], there, seq_sem.at[step], at.seq_peer(step), lambda: dx.at[:, pl.ds(0, tokens)])
        if number == 1:
            vec_take(0)
            vec_hop(1, at.x_peer)
    own_dx = pltpu.make_async_copy(dx.at[:, mine], dx_own.at[pl.ds(at.seq * seqs, seqs)], own_sem.at[0])
    own_dx.start()
    vec_take(1)
    vec_hop(2, at.y_peer)
    reduce_at(units + 4)
    vec_take(2)
    vec_in[2 * n_z + 2] = vec_out[...]
    for step in range(1, n_z):
        sends.start(vec_in.at[2 * n_z + 2], vec_in.at[2 + 2 * n_z + step], vec_sem.at[3 + step], at.z_peer(step))
    reduce_at(units + 5)
    for step in range(1, n_z):
        slot_in = 2 + 2 * n_z + step
        sends.arrived(vec_in.at[slot_in], vec_sem.at[3 + step], at.core_peer)
        vec_out[...] = vec_out[...] + vec_in[slot_in]
    for step in (1, 2, 3):
        theirs = pl.ds(at.seq_at(4 - step) * seqs, seqs)
        sends.arrived(dx_own.at[theirs], seq_sem.at[step], at.core_peer)
    own_dx.wait()
    sends.drain(at.core_peer)


def finish(n_batch, mask, qkv, att, datt, lse, x, mats, dr1, act_t, du, h1_t, dz, da, sums):
    _, _, depth, _ = mats.shape
    rows = 3 * depth
    length = mask.shape[1]
    n_z = n_batch // 2
    seqs = att.shape[0]
    whole = (att.shape, BF16)
    turned = (D, seqs * length)
    vec = (sum(VEC_LENGTHS) // 128, 128)
    vmem = [
        (qkv.shape, BF16),
        whole,
        whole,
        (lse.shape, F32),
        ((3, D, D), BF16),
        (att.shape, F32),
        (qkv.shape, BF16),
        whole,
        (turned, BF16),
        ((2,) + turned, BF16),
        ((2, length, length), jnp.int32),
        ((length, length), BF16),
        ((length, length), BF16),
        ((4, n_batch, rows, D), BF16),
        ((2, n_batch, rows, D), BF16),
        ((n_batch, rows, D), BF16),
        ((2, 2, n_z, rows, D), BF16),
        ((rows, D), BF16),
        ((3 * n_z + 3,) + vec, F32),
    ]
    sems = [(9 + n_batch,), (2,), (2,), (2,), (1,), (400,), (2, n_batch, 3), (n_batch,), (2, 2, n_z, 3), (3,), (n_z + 3,), (4,)]
    return pl.pallas_call(
        functools.partial(finish_kernel, n_batch),
        out_shape=(
            jax.ShapeDtypeStruct((rows, D), F32),
            jax.ShapeDtypeStruct(vec, F32),
            jax.ShapeDtypeStruct((seqs * 4, length // 4, D), BF16),
        ),
        in_specs=[ANY] * 13 + [VMEM],
        out_specs=[VMEM, VMEM, ANY],
        scratch_shapes=[pltpu.VMEM(shape, dtype) for shape, dtype in vmem]
        + [pltpu.SemaphoreType.DMA(shape) for shape in sems],
        compiler_params=pltpu.CompilerParams(
            collective_id=1, has_side_effects=True, vmem_limit_bytes=62 * MIB
        ),
        name="finish",
    )(mask, qkv, att, datt, lse, x, mats, dr1, act_t, du, h1_t, dz, da, sums)


def attention(qkv, mask):
    heads = mask.shape[0]
    q, k, v = (part.reshape(part.shape[:2] + (heads, D // heads)) for part in qkv)
    scores = jnp.einsum("bqhd,bkhd->bhqk", q, k, preferred_element_type=F32) / math.sqrt(D // heads)
    scores = jnp.where(mask > 0, scores, NEG_FILL)
    largest = jnp.max(scores, -1, keepdims=True)
    expo = jnp.exp(scores - largest)
    total = jnp.sum(expo, -1, keepdims=True)
    probs = (expo / total).astype(BF16)
    mixed = jnp.einsum("bhqk,bkhd->bqhd", probs, v, preferred_element_type=F32)
    return mixed.astype(BF16).reshape(qkv.shape[1:])


def middle_plain(mats, vecs, x, att, dy):
    pieces, offset = [], 0
    for size in VEC_LENGTHS:
        pieces.append(vecs.reshape(-1)[offset : offset + size])
        offset += size
    _, _, b_o, b_1, b_2, g_1, s_1, g_2, s_2 = pieces
    w_out, w_down = (take_matrix(mats, name)[0] for name in ("out", "down"))
    w_up = take_matrix(mats, "up").swapaxes(0, 1).reshape(D, FF)
    r1 = x.astype(F32) + jnp.dot(att, w_out, preferred_element_type=F32) + b_o
    h1 = layer_norm(r1, g_1, s_1)
    h1_low = h1.astype(BF16)
    up = jnp.dot(h1_low, w_up, preferred_element_type=F32) + b_1
    act = gelu_exact(up).astype(BF16)
    r2 = h1 + jnp.dot(act, w_down, preferred_element_type=F32) + b_2
    out = layer_norm(r2, g_2, s_2).astype(BF16)
    _, norm_two_back = jax.vjp(layer_norm, r2, g_2, s_2)
    dr2, dg_2, ds_2 = norm_two_back(dy.astype(F32))
    dz = dr2.astype(BF16)
    _, gelu_back = jax.vjp(gelu_exact, up)
    du = gelu_back(contract_cols(dz, w_down))[0].astype(BF16)
    dh1 = dr2 + contract_cols(du, w_up)
    _, norm_one_back = jax.vjp(layer_norm, r1, g_1, s_1)
    dr1, dg_1, ds_1 = norm_one_back(dh1)
    da = dr1.astype(BF16)
    datt = contract_cols(da, w_out).astype(BF16)
    mats_grad = {
        "out": contract_rows(att, da)[None],
        "up": contract_rows(h1_low, du).reshape(D, FF // D, D).swapaxes(0, 1),
        "down": contract_rows(act, dz)[None],
    }
    sums = [jnp.sum(member.astype(F32), 0) for member in (da, du, dz)]
    return out, dr1, datt, mats_grad, jnp.concatenate(sums + [dg_1, ds_1, dg_2, ds_2])


def finish_plain(mask, qkv, datt, x, w_qkv, dr1):
    heads = mask.shape[0]
    seqs, length, _ = x.shape
    split = (seqs, length, heads, D // heads)
    q, k, v = (part.reshape(split) for part in qkv)
    g = datt.reshape(split)
    scale = 1.0 / math.sqrt(D // heads)
    scores = jnp.einsum("bqhd,bkhd->bhqk", q, k, preferred_element_type=F32) * scale
    probs = jax.nn.softmax(jnp.where(mask > 0, scores, NEG_FILL), -1)
    dprobs = jnp.einsum("bqhd,bkhd->bhqk", g, v, preferred_element_type=F32)
    inner = jnp.sum(probs * dprobs, -1, keepdims=True)
    dscore = (probs * (dprobs - inner)).astype(BF16)
    dq = jnp.einsum("bhqk,bkhd->bqhd", dscore, k, preferred_element_type=F32) * scale
    dk = jnp.einsum("bhqk,bqhd->bkhd", dscore, q, preferred_element_type=F32) * scale
    dv = jnp.einsum("bhqk,bqhd->bkhd", probs.astype(BF16), g, preferred_element_type=F32)
    dqkv = jnp.stack([dq, dk, dv]).astype(BF16).reshape(3, seqs * length, D)
    dw = jnp.stack([contract_rows(x.reshape(-1, D), part) for part in dqkv])
    dx = dr1 + sum(contract_cols(dqkv[j], w_qkv[j]) for j in range(3))
    db = [jnp.sum(dqkv[j].astype(F32), 0) for j in (0, 2)]
    return dw, dx.astype(BF16).reshape(x.shape), jnp.concatenate(db)


def local(
    n_batch,
    inputs,
    out_grad,
    out_mask,
    attn_mask,
    mat_param,
    mat_first,
    mat_second,
    vec_param,
    vec_first,
    vec_second,
):
    shares = 4 * n_batch
    share_rows = mat_param.shape[0] // D
    vec_len = vec_param.shape[0]
    me = lax.axis_index("seq") * n_batch + lax.axis_index("batch")

    share = rearrange(me, shares, mat_param.reshape(share_rows, D).astype(BF16), by_columns)
    vec_share = lax.dynamic_update_slice(
        jnp.zeros((shares * vec_len,), F32), vec_param.astype(BF16).astype(F32), (me * vec_len,)
    ).reshape(-1, 128)
    if share_rows % 96 == 0 and share_rows * n_batch == 3 * D:
        mats, x_all, qkv, attended, lse, outputs, *middle = forward(
            n_batch, share, vec_share, inputs, out_grad, out_mask, attn_mask
        )
        dr1, datt, *middle = middle
        mat_grad, vec_sum, dx = finish(n_batch, attn_mask, qkv, attended, datt, lse, x_all, mats, dr1, *middle)
        vec_grad = lax.dynamic_slice_in_dim(vec_sum.reshape(-1), me * vec_len, vec_len)
    else:
        mats = lax.all_gather(share, ("seq", "batch"))
        vecs = lax.psum(vec_share, ("seq", "batch")).reshape(-1)
        dy_low = (out_grad * out_mask[..., None].astype(F32)).astype(BF16)
        x_all, dy_all = (
            lax.all_to_all(member, "seq", 0, 1, tiled=True) for member in (inputs, dy_low)
        )
        whole = x_all.shape
        flat = (whole[0] * whole[1], D)
        w_qkv = regroup(take_matrix(mats, "qkv"))
        proj = jnp.stack([jnp.dot(x_all.reshape(flat), part, preferred_element_type=F32) for part in w_qkv])
        proj = proj + jnp.stack([vecs[:D], jnp.zeros((D,), F32), vecs[D : 2 * D]])[:, None]
        qkv = proj.astype(BF16).reshape((3,) + whole)
        attended = attention(qkv, attn_mask).reshape(flat)
        out_all, dr1, datt, mats_grad, grad_vecs = middle_plain(
            mats, vecs, x_all.reshape(flat), attended, dy_all.reshape(flat)
        )
        mats_grad["qkv"], dx_all, db = finish_plain(attn_mask, qkv, datt, x_all, w_qkv, dr1)
        mats_grad["qkv"] = regroup(mats_grad["qkv"])
        grads = to_shares({name: part.astype(BF16) for name, part in mats_grad.items()}, shares)
        mat_grad = lax.psum_scatter(grads.astype(F32), ("seq", "batch"))
        vec_grad = lax.psum_scatter(jnp.concatenate([db, grad_vecs]), ("seq", "batch"), tiled=True)
        outputs, dx = (
            lax.all_to_all(member, "seq", 1, 0, tiled=True) for member in (out_all.reshape(whole), dx_all)
        )
    mat_grad = rearrange(me, shares, mat_grad, by_rows).reshape(-1)
    return (
        outputs,
        dx.astype(F32),
        *adam_step(mat_param, mat_first, mat_second, mat_grad, MATS_RATE),
        *adam_step(vec_param, vec_first, vec_second, vec_grad, VECS_RATE),
    )


def solution(mesh):
    flat = P(("seq", "batch"))
    tokens = P("batch", "seq", None)
    return jax.shard_map(
        functools.partial(local, mesh.shape["batch"]),
        mesh=mesh,
        in_specs=(tokens, tokens, P("batch", "seq"), P()) + (flat,) * 6,
        out_specs=(tokens, tokens) + (flat,) * 6,
        check_vma=False,
    )
```

```python
import functools
import math

import jax
import jax.numpy as jnp
from jax import lax
from jax.experimental import pallas as pl
from jax.experimental.pallas import tpu as pltpu
from jax.sharding import PartitionSpec as P

D = 768
FF = 3072
STEP = 10


NEG_FILL = -1e30
NORM_EPS = 1e-06
ROOT_HALF = 0.7071067811865476
ROOT_TWO_PI_INV = 0.3989422804014327
BETA_ONE = 0.9
BETA_TWO = 0.999
ADAM_EPS = 1e-08
DECAY_RATE = 0.01
MATS_RATE = 0.1
VECS_RATE = 0.5

BF16 = jnp.bfloat16
F32 = jnp.float32
MESH = pl.DeviceIdType.MESH
ANY = pl.BlockSpec(memory_space=pl.ANY)
VMEM = pl.BlockSpec(memory_space=pltpu.VMEM)
MIB = 1 << 20

MATRICES = (("qkv", 3 * D, 3), ("out", D, 1), ("up", FF, FF // D), ("down", FF, 1))
VEC_LENGTHS = (D, D, D, FF, D, D, D, D, D)


def layer_norm(values, gain, shift):
    center = values - jnp.mean(values, -1, keepdims=True)
    spread = jnp.mean(center * center, -1, keepdims=True)
    return center * lax.rsqrt(spread + NORM_EPS) * gain + shift


def gelu_exact(values):
    return 0.5 * values * (1.0 + lax.erf(values * ROOT_HALF))


def adam_step(param, first, second, grad, rate):
    first_new = BETA_ONE * first + (1.0 - BETA_ONE) * grad
    second_new = BETA_TWO * second + (1.0 - BETA_TWO) * grad * grad
    first_hat = first_new / (1.0 - BETA_ONE**STEP)
    second_hat = second_new / (1.0 - BETA_TWO**STEP)
    param_new = param - rate * (first_hat / (jnp.sqrt(second_hat) + ADAM_EPS) + DECAY_RATE * param)
    return (param_new, first_new, second_new)


def contract_rows(operand_one, operand_two):
    return lax.dot_general(
        operand_one, operand_two, (((0,), (0,)), ((), ())), preferred_element_type=jnp.float32
    )


def contract_cols(operand_one, operand_two):
    return lax.dot_general(
        operand_one, operand_two, (((1,), (1,)), ((), ())), preferred_element_type=jnp.float32
    )


def segments(share, rows):
    found, start = [], 0
    for name, length, pieces in MATRICES:
        low, high = max(start, share * rows), min(start + length, (share + 1) * rows)
        if low < high:
            found.append((name, pieces, low - share * rows, low - start, high - low))
        start += length
    return found


def by_columns(name, block, pieces):
    rows = block.shape[0]
    if name == "qkv":
        return block.reshape(rows // 3, 3, 3, D // 3).transpose(2, 0, 1, 3).reshape(rows, D)
    return block.reshape(rows // pieces, pieces, D).swapaxes(0, 1).reshape(rows, D)


def by_rows(name, block, pieces):
    rows = block.shape[0]
    if name == "qkv":
        return block.reshape(3, rows // 3, 3, D // 3).transpose(1, 2, 0, 3).reshape(rows, D)
    return block.reshape(pieces, rows // pieces, D).swapaxes(0, 1).reshape(rows, D)


def regroup(blocks):
    return blocks.reshape(3, D, 3, D // 3).transpose(2, 1, 0, 3).reshape(3, D, D)


def rearrange(share_index, shares, block, change):
    rows = block.shape[0]
    layouts, starts = [], []
    for share in range(shares):
        layout = tuple((name, pieces, at, size) for name, pieces, at, _, size in segments(share, rows))
        if not layouts or layout != layouts[-1]:
            layouts.append(layout)
            starts.append(share)

    def branch(layout, values):
        return jnp.concatenate([change(name, values[at : at + size], pieces) for name, pieces, at, size in layout])

    return lax.switch(
        sum((share_index >= start).astype(jnp.int32) for start in starts[1:]),
        [functools.partial(branch, layout) for layout in layouts],
        block,
    )


def take_matrix(gathered, name):
    shares, rows, _ = gathered.shape
    found = []
    for share in range(shares):
        for other, pieces, at, _, size in segments(share, rows):
            if other == name:
                found.append(gathered[share, at : at + size].reshape(pieces, size // pieces, D))
    return jnp.concatenate(found, 1)


def to_shares(blocks, shares):
    rows = sum(length for _, length, _ in MATRICES) // shares
    found = []
    for share in range(shares):
        for name, pieces, _, begin, size in segments(share, rows):
            part = blocks[name][:, begin // pieces : (begin + size) // pieces]
            found.append(part.reshape(size, D))
    return jnp.concatenate(found).reshape(shares, rows, D)


class Place:
    def __init__(self, n_batch):
        self.n_batch, self.n_z = n_batch, n_batch // 2
        self.seq, self.batch = lax.axis_index("seq"), lax.axis_index("batch")
        self.x, self.core = self.seq // 2, self.seq % 2
        self.z, self.y = self.batch // 2, self.batch % 2
        self.x_peer = {"seq": (1 - self.x) * 2 + self.core}
        self.core_peer = {"seq": self.x * 2 + 1 - self.core}
        self.y_peer = {"batch": self.z * 2 + 1 - self.y}
        self.ring = 2 * self.n_z
        self.position = (1 - self.y) * self.z + self.y * (self.ring - 1 - self.z)
        self.next, self.prev = {"batch": self.around(1)}, {"batch": self.around(-1)}

    def around(self, step):
        place = (self.position + step + self.ring) % self.ring
        y = place // self.n_z
        return 2 * ((1 - y) * place + y * (self.ring - 1 - place)) + y

    def share(self, x, core, step):
        return (2 * x + core) * self.n_batch + self.around(step)

    def z_at(self, step):
        return (self.z + step) % self.n_z

    def z_peer(self, step):
        return {"batch": self.z_at(step) * 2 + self.y}

    def seq_at(self, step):
        return (self.seq + step) % 4

    def seq_peer(self, step):
        return {"seq": self.seq_at(step)}

    def barrier(self):
        barrier = pltpu.get_barrier_semaphore()
        peers = [self.seq_peer(step) for step in (1, 2, 3)]
        peers += [self.y_peer] + [self.z_peer(step) for step in range(1, self.n_z)]
        for peer in peers:
            pl.semaphore_signal(barrier, inc=1, device_id=peer, device_id_type=MESH)
        pl.semaphore_wait(barrier, len(peers))


def run(steps):
    for step in steps:
        step()


def dispatch(now, steps, body):
    if len(steps) == 1:
        pl.when(now == steps[0])(functools.partial(body, steps[0]))
    elif steps:
        middle = len(steps) // 2
        lax.cond(
            now < steps[middle],
            lambda: dispatch(now, steps[:middle], body),
            lambda: dispatch(now, steps[middle:], body),
        )


def share_layouts(shares, rows):
    found = []
    for share in range(shares):
        layout = [(name, pieces, at, size) for name, pieces, at, _, size in segments(share, rows)]
        if not found or found[-1][1] != layout:
            found.append((share, layout))
    return found


def for_share(number, shares, rows, body):
    layouts = share_layouts(shares, rows)
    for (begin, layout), end in zip(layouts, [begin for begin, _ in layouts[1:]] + [shares]):
        pl.when(jnp.logical_and(number >= begin, number < end))(functools.partial(body, layout))


def share_blocks(layout):
    per = D // 128
    for name, pieces, at, size in layout:
        each = size // pieces
        for j in range(pieces):
            for k in range(per):
                flat = pl.ds((at + j) * per + k, each, stride=per * pieces)
                if name == "qkv":
                    row, column = at + k // 2 * each, j * (D // 3) + k % 2 * 128
                else:
                    row, column = at + j * each, k * 128
                yield flat, slice(row, row + each), slice(column, column + 128)


class Sends:
    def __init__(self, sems):
        self.sems, self.started, self.when = sems, [], None

    def start(self, src, dst, recv_sem, peer, like=None):
        copy = pltpu.make_async_remote_copy(
            src_ref=src,
            dst_ref=dst,
            send_sem=self.sems.at[len(self.started)],
            recv_sem=recv_sem,
            device_id=peer,
            device_id_type=MESH,
        )
        copy.start()
        self.started.append((self.when, like or (lambda: src)))

    def arrived(self, dst, recv_sem, peer):
        pltpu.make_async_remote_copy(
            src_ref=dst,
            dst_ref=dst,
            send_sem=self.sems.at[0],
            recv_sem=recv_sem,
            device_id=peer,
            device_id_type=MESH,
        ).wait_recv()

    def sent(self, last, count, peer):
        for index in range(len(self.started) - last, len(self.started) - last + count):
            self.wait(index, self.started[index][1](), peer)
            self.started[index] = None

    def wait(self, index, ref, peer):
        pltpu.make_async_remote_copy(
            src_ref=ref,
            dst_ref=ref,
            send_sem=self.sems.at[index],
            recv_sem=self.sems.at[index],
            device_id=peer,
            device_id_type=MESH,
        ).wait_send()

    def under(self, condition, body):
        outer = self.when
        self.when = condition if outer is None else jnp.logical_and(outer, condition)

        @pl.when(condition)
        def _():
            body()

        self.when = outer

    def drain(self, peer):
        assert len(self.started) <= self.sems.shape[0]
        for index, (when, like) in [(i, one) for i, one in enumerate(self.started) if one]:
            if when is None:
                self.wait(index, like(), peer)
            else:
                pl.when(when)(lambda: self.wait(index, like(), peer))


def contract(one, two, dims):
    return lax.dot_general(one, two, ((dims[:1], dims[1:]), ((), ())), preferred_element_type=F32)


def half_of(shape, head):
    return lax.broadcasted_iota(jnp.int32, shape, 1) // 64 == head % 2


def row_of(grid, first, count):
    return jnp.concatenate([grid[first + i : first + i + 1, :] for i in range(count)], 1)


def attend_head(head, seq, qkv, mask, att, lse):
    lanes = pl.ds(pl.multiple_of(head // 2 * 128, 128), 128)
    length = mask.shape[0]
    block = 256
    k = qkv[1, seq, :, lanes]
    v = qkv[2, seq, :, lanes]
    v = jnp.where(half_of(v.shape, head), v, 1.0).astype(BF16)
    for i in range(length // block):
        rows = pl.ds(i * block, block)
        q = qkv[0, seq, rows, lanes]
        q = jnp.where(half_of(q.shape, head), q * 0.125, 0.0).astype(BF16)
        scores = contract(q, k, (1, 1))
        scores = jnp.where(mask[rows, :] > 0, scores, NEG_FILL)
        largest = jnp.max(scores, -1, keepdims=True)
        both = contract(jnp.exp(scores - largest).astype(BF16), v, (1, 0))
        turned = pltpu.roll(both, 64, 1)
        old = att[seq, rows, lanes]
        att[seq, rows, lanes] = jnp.where(half_of(old.shape, head), (both / turned).astype(BF16), old)
        total = jnp.where(head % 2 == 0, turned, both)
        kept = lse[seq, rows, :]
        lane = lax.broadcasted_iota(jnp.int32, kept.shape, 1)
        lse[seq, rows, :] = jnp.where(lane == head, largest + jnp.log(total), kept)


def head_backward(head, seq, qkv, mask, att, datt, lse, probs, dscore, dqkv):
    lanes = pl.ds(pl.multiple_of(head // 2 * 128, 128), 128)
    length = mask.shape[0]
    block = 256
    k = qkv[1, seq, :, lanes]
    v = qkv[2, seq, :, lanes]
    own = half_of(k.shape, head)
    k_own = jnp.where(own, k, 0.0).astype(BF16)
    for i in range(length // block):
        rows = pl.ds(i * block, block)
        q = qkv[0, seq, rows, lanes]
        g = datt[seq, rows, lanes]
        half = half_of(q.shape, head)
        q = jnp.where(half, q * 0.125, 0.0).astype(BF16)
        g = jnp.where(half, g, 0.0).astype(BF16)
        kept = lse[seq, rows, :]
        lane = lax.broadcasted_iota(jnp.int32, kept.shape, 1)
        total = jnp.sum(jnp.where(lane == head, kept, 0.0), -1, keepdims=True)
        inner = jnp.sum(g.astype(F32) * att[seq, rows, lanes].astype(F32), -1, keepdims=True)
        scores = contract(q, k, (1, 1))
        p = jnp.where(mask[rows, :] > 0, jnp.exp(scores - total), 0.0)
        d = p * (contract(g, v, (1, 1)) - inner)
        probs[rows, :] = p.astype(BF16)
        d = d.astype(BF16)
        dscore[rows, :] = d
        dq = contract(d, k_own, (1, 0)) * 0.125
        old = dqkv[0, seq, rows, lanes]
        dqkv[0, seq, rows, lanes] = jnp.where(half, dq.astype(BF16), old)
    q = qkv[0, seq, :, lanes]
    g = datt[seq, :, lanes]
    dk = contract(q.T, dscore[...], (1, 0)).T * 0.125
    dv = contract(g.T, probs[...], (1, 0)).T
    for j, value in ((1, dk), (2, dv)):
        old = dqkv[j, seq, :, lanes]
        dqkv[j, seq, :, lanes] = jnp.where(own, value.astype(BF16), old)


def add_rows(target, target_rows, *others):
    step = 32
    first, size = target_rows

    def body(i, carry):
        at = pl.ds(pl.multiple_of(first + i * step, 16), step)
        total = target[at].astype(F32)
        for ref, begin in others:
            total = total + ref[pl.ds(pl.multiple_of(begin + i * step, 16), step)].astype(F32)
        target[at] = total.astype(target.dtype)
        return carry

    lax.fori_loop(0, size // step, body, 0)


def norm_parts(values):
    center = values - jnp.mean(values, -1, keepdims=True)
    scale = lax.rsqrt(jnp.mean(center * center, -1, keepdims=True) + NORM_EPS)
    return center * scale, scale


def norm_back(grad, normed, scale, gain):
    dn = grad * gain
    along = jnp.mean(dn * normed, -1, keepdims=True)
    return (dn - jnp.mean(dn, -1, keepdims=True) - normed * along) * scale


BEFORE_UP, LAST_STEP = 72, 89
ACROSS_ORDER = (0, 1, -1, 2, -2, 3, -3, 4)
FIRST = {
    0: (("q", 1, 0), ("q_start", 1), ("q", 2, 0), ("q", 1, 1), ("q_start", 2), ("q", 3, 0), ("q", 2, 1), ("q", 1, 2), ("q", 4, 0)),
    2: (("q", 1, 0), ("q", 2, 0), ("q_start", 1), ("q", 3, 0), ("q", 1, 1), ("q", 4, 0)),
}
THEN = {
    0: (("q", 3, 1), ("q", 2, 2), ("q", 4, 1), ("q", 3, 2), ("q", 4, 2)),
    2: (("q", 2, 1), ("q_start", 2), ("q", 3, 1), ("q", 1, 2), ("q", 4, 1), ("q", 2, 2), ("q", 3, 2), ("q", 4, 2)),
}
TIMES = {
    0: dict(then=(0, 15, 27, 69, 84), far=(28, 36, 52, 68, 79), across=(11, 17, 32, 33, 77), dy=27),
    1: dict(own=(3, 18, 29, 33, 49), over_x=4, far=(30, 47, 64, 76, 82), dy=23),
    2: dict(then=(0, 2, 3, 6, 13, 13, 67, 71), own=(-1, 26, 42, 52, 60), over_x=0, dy=63),
    3: dict(own=(21, 66, 73, 84, 89), over_x=17, far=(9, 38, 53, 63, 75), across=(0, 0, 7, 11, 82), dy=72),
}


def timetable():
    found = []

    def put(seq, step, rank, limit, *what):
        found.append((min(step, limit), rank, len(found), seq, what))

    for seq, times in TIMES.items():
        put(seq, -1, 0, -1, "x", 1)
        group = 1
        for step, what in zip(times.get("then", ()), THEN.get(seq, ())):
            put(seq, step, 1, 12 * group - 1, *what)
            group += what == ("q", 4, 1)
        if seq % 2:
            for piece in (1, 2):
                put(seq, 12 * piece, 1, LAST_STEP, "q_from_core", piece)
        limit = LAST_STEP if seq == 3 else BEFORE_UP
        if "own" in times:
            for rank, (step, what) in enumerate(zip(times["own"], (("start",), *(("own", hops) for hops in range(1, 5))))):
                put(seq, step, 2 + (rank > 0), limit, *what)
            put(seq, times["over_x"], 2, limit, "over_x")
        limit = LAST_STEP if seq == 1 else BEFORE_UP
        if "far" in times:
            for rank, (step, what) in enumerate(zip(times["far"], (("far_start",), *(("far", hops) for hops in range(1, 5))))):
                put(seq, step, 4 + (rank > 0), limit, *what)
        if "across" in times:
            for i, place in enumerate(ACROSS_ORDER):
                step = max(times["across"][(i + 1) // 2], times["far"][abs(place)])
                put(seq, step, 6, BEFORE_UP, "across", place)
        put(seq, times["dy"], 7, LAST_STEP, "dy")
    table = {}
    for step, _, _, seq, what in sorted(found):
        table.setdefault((seq, step), []).append(what)
    return table


def forward_kernel(
    n_batch, plan, flat, vec, x_in, grad_in, scored, mask,
    mats, x_out, qkv_out, att_out, lse_out, out_own, dr1_out, datt_out, act_out, du_out, h1_out, dz_out, da_out, sums,
    x_all, att, dy, dy_in, out, share_wide, share, wide, datt, w_out, w_up, w_down, stage, act, act_t, slope, h1_t, dz, da, scales, biases, lse, masks, vecs, vec_in,
    own_sem, send_sem, mat_sem, vec_sem, seq_sem, w_sem, mask_sem, out_sem, load_sem, stage_sem, row_sem, give_sem, give_own, grad_sem,
):
    at = Place(n_batch)
    n_z, tokens = at.n_z, x_in.shape[1]
    half = at.ring // 2
    me = at.share(at.x, at.core, 0)
    sends = Sends(send_sem)
    heads = mask.shape[0]
    seqs, length = x_all.shape[:2]
    depth = share.shape[1]
    n_up = FF // D
    shares = mats.shape[0]
    mine = pl.ds(at.seq * tokens, tokens)
    w, qkv = w_up, slope

    own = [
        pltpu.make_async_copy(share, mats.at[me], own_sem.at[0]),
        pltpu.make_async_copy(x_in.at[pl.ds(at.seq * seqs, seqs)], x_all.at[:, mine], own_sem.at[1]),
        pltpu.make_async_copy(dy_in.at[pl.ds(at.seq * seqs, seqs)], dy.at[:, mine], own_sem.at[2]),
    ]
    per_row = length // tokens
    grads = []
    for i in range(grad_in.shape[0]):
        there = wide.at[i // per_row, pl.ds(i % per_row * tokens, tokens)]
        grads.append(pltpu.make_async_copy(grad_in.at[i], there, grad_sem.at[i]))
    for copy in own[1:2] + grads:
        copy.start()

    for unit in range(2):
        pltpu.make_async_copy(mask.at[unit], masks.at[unit], mask_sem.at[unit]).start()
    vecs[...] = vec[...]

    def from_flat_order(layout):
        for flat_rows, lines, lanes in share_blocks(layout):
            share_wide[lines, lanes] = flat[flat_rows, :]

    for_share(at.seq * n_batch + at.batch, shares, 3 * depth, from_flat_order)
    for piece in range(3):
        share[piece] = share_wide[piece * depth : (piece + 1) * depth, :].astype(BF16)
    own[0].start()
    at.barrier()

    all_of = (0, 3, 0)
    first_of, rest_of = (0, 1, 0), (1, 3, 2)
    whole_ring = (all_of, ((0, 1, 0), (1, 3, 1)))
    rest_ring = (rest_of, ((1, 2, 1), (2, 3, 2)))

    def piece_ring(piece):
        part = (piece, piece + 1, piece)
        return (part, (part, None) if piece == 0 else (None, part))

    def part_at(index, part):
        return mats.at[index, pl.ds(part[0], part[1] - part[0])]

    def wait(index, part):
        sends.arrived(part_at(index, part), mat_sem.at[index, part[2]], at.core_peer)

    def pass_on(index, part, *peers):
        for peer in peers:
            sends.start(part_at(index, part), part_at(index, part), mat_sem.at[index, part[2]], peer, lambda: part_at(0, part))

    def lay_out(index, piece):
        rows = pl.ds(pl.multiple_of(index * depth, 32), depth)
        return pltpu.make_async_copy(mats.at[index, piece], w.at[piece, rows], w_sem.at[index, piece])

    def nothing(index):
        pass

    def round_start(x_at, ring):
        pass_on(at.share(x_at, at.core, 0), ring[0], at.next, at.prev)

    def round_step(x_at, hops, ring, then):
        for way, sign, peer in ((0, -1, at.next), (1, 1, at.prev)):
            index = at.share(x_at, at.core, sign * hops)
            part = ring[0] if hops < half else ring[1][way]
            if part:
                wait(index, part)
            onward = ring[0] if hops < half - 1 else ring[1][way] if hops == half - 1 else None
            if onward:
                pass_on(index, onward, peer)
            if hops < half:
                then(index)
        if hops == half:
            then(at.share(x_at, at.core, half))

    def vec_hop(hop, peer):
        vec_in[hop + n_z] = vecs[...]
        sends.start(vec_in.at[hop + n_z], vec_in.at[hop], vec_sem.at[hop], peer)

    def vec_take(hop):
        sends.arrived(vec_in.at[hop], vec_sem.at[hop], at.core_peer)
        vecs[...] = vecs[...] + vec_in[hop]

    def exchange(src, dst, which, seq):
        for step in (1, 2, 3):
            theirs = at.seq_at(step) * seqs + seq
            sends.start(src.at[theirs], dst.at[seq, mine], seq_sem.at[which, seq, step], at.seq_peer(step), lambda: src.at[0])

    def exchanged(dst, which, seq):
        for step in (1, 2, 3):
            theirs = pl.ds(at.seq_at(4 - step) * tokens, tokens)
            sends.arrived(dst.at[seq, theirs], seq_sem.at[which, seq, step], at.core_peer)

    is_class = [at.seq == seq for seq in range(4)]
    is_core0, is_core1 = at.core == 0, at.core == 1
    vec_hop(0, at.core_peer)
    own[0].wait()

    def q_arrived(piece, index):
        pass_on(index, piece_ring(piece)[0], at.core_peer)
        lay_out(index, piece).start()

    def q_start(seq, piece):
        index = at.share(0, 0, 0)
        if seq == 2:
            wait(index, piece_ring(piece)[0])
        round_start(0, piece_ring(piece))
        q_arrived(piece, index)

    def q_step(hops, piece):
        round_step(0, hops, piece_ring(piece), functools.partial(q_arrived, piece))

    def q_from_core(piece, first=0):
        for hops in range(first, half + 1):
            for sign in (-1, 1) if 0 < hops < half else (1,):
                index = at.share(0, 0, sign * hops)
                wait(index, piece_ring(piece)[0])
                lay_out(index, piece).start()

    def other_start(seq):
        round_start(at.x, whole_ring)
        pass_on(me, all_of, at.core_peer)

    def own_over_x(seq):
        if seq == 3:
            pass_on(me, all_of, at.x_peer)
        else:
            pass_on(me, rest_of, at.x_peer)
            pass_on(me, first_of, at.x_peer)

    def own_arrived(seq, index):
        if seq != 3:
            pass_on(index, first_of, at.x_peer)
        pass_on(index, all_of, at.core_peer)

    def far_arrived(index):
        pass_on(index, all_of, at.core_peer)

    def far_start(seq):
        index = at.share(1 - at.x, at.core, 0)
        ring = whole_ring if seq == 1 else rest_ring
        wait(index, ring[0])
        round_start(1 - at.x, ring)
        if seq == 1:
            far_arrived(index)

    def far_step(seq, hops):
        if seq == 1:
            round_step(1 - at.x, hops, whole_ring, far_arrived)
        else:
            round_step(1 - at.x, hops, rest_ring, nothing)

    def across(place):
        index = at.share(1 - at.x, at.core, place)
        wait(index, first_of)
        far_arrived(index)

    def relay(seq, what, *which):
        if what == "q":
            q_step(*which)
        elif what == "q_start":
            q_start(seq, *which)
        elif what == "q_from_core":
            q_from_core(*which)
        elif what == "start":
            other_start(seq)
        elif what == "over_x":
            own_over_x(seq)
        elif what == "own":
            round_step(at.x, *which, whole_ring, functools.partial(own_arrived, seq))
        elif what == "far_start":
            far_start(seq)
        elif what == "far":
            far_step(seq, *which)
        elif what == "across":
            across(*which)
        elif what == "x":
            exchange(x_in, x_all, 0, *which)
        else:
            for number in range(seqs):
                exchange(dy_in, dy, 1, number)

    def relay_all(seq, some):
        sends.under(is_class[seq], lambda: run([functools.partial(relay, seq, *one) for one in some]))

    def first_of_class0():
        pass_on(me, piece_ring(0)[0], at.x_peer)
        q_start(0, 0)
        sends.sent(4, 1, at.x_peer)
        exchange(x_in, x_all, 0, 0)
        for piece in (1, 2):
            pass_on(me, piece_ring(piece)[0], at.x_peer)

    def first_of_class1():
        index = at.share(0, 0, 0)
        wait(index, piece_ring(0)[0])
        lay_out(index, 0).start()
        exchange(x_in, x_all, 0, 0)

    def first_of_class2():
        exchange(x_in, x_all, 0, 0)
        q_start(2, 0)

    def first_of_class3():
        exchange(x_in, x_all, 0, 0)

    for seq, first in enumerate((first_of_class0, first_of_class1, first_of_class2, first_of_class3)):
        sends.under(is_class[seq], first)
    square = (tokens, tokens)
    diagonal = lax.broadcasted_iota(jnp.int32, square, 0) == lax.broadcasted_iota(jnp.int32, square, 1)
    for i, copy in enumerate(grads):
        copy.wait()
        column = jnp.sum(jnp.where(diagonal, scored[i : i + 1, :].astype(F32), 0.0), -1, keepdims=True)
        dy_in[i] = (wide[i // per_row, i % per_row * tokens : (i % per_row + 1) * tokens] * column).astype(BF16)
    own[2].start()
    vec_take(0)
    vec_hop(1, at.x_peer)
    for seq in (0, 2):
        relay_all(seq, FIRST[seq][:3])
    vec_take(1)
    vec_hop(2, at.y_peer)
    for seq in (0, 2):
        relay_all(seq, FIRST[seq][3:])
    sends.under(is_class[1], lambda: q_from_core(0, 1))
    sends.under(is_class[3], lambda: q_from_core(0))
    vec_take(2)
    vec_in[2 * n_z + 2] = vecs[...]
    for step in range(1, n_z):
        sends.start(vec_in.at[2 * n_z + 2], vec_in.at[2 + 2 * n_z + step], vec_sem.at[3 + step], at.z_peer(step))

    table = timetable()

    def relays(step):
        for seq in range(4):
            if (seq, step) in table:
                relay_all(seq, table[seq, step])

    def relays_in_loop(now, first, each, count):
        def turn(number):
            for step in range(first + number * each, first + (number + 1) * each):
                relays(step)

        held = {(step - first) // each for _, step in table if first <= step < first + each * count}
        dispatch(now, sorted(held), turn)

    relays(-1)
    for step in range(1, n_z):
        slot_in = 2 + 2 * n_z + step
        sends.arrived(vec_in.at[slot_in], vec_sem.at[3 + step], at.core_peer)
        vecs[...] = vecs[...] + vec_in[slot_in]
    exchanged(x_all, 0, 0)
    own[1].wait()

    grid = vecs[...]
    per = D // 128
    starts, offset = [], 0
    for size in VEC_LENGTHS:
        starts.append(offset // 128)
        offset += size
    width = D // 3
    b_q, b_v = row_of(grid, 0, per), row_of(grid, per, per)
    for piece in range(3):
        part = slice(piece * width, (piece + 1) * width)
        biases[piece, 0:1] = jnp.concatenate([b_q[:, part], jnp.zeros((1, width), F32), b_v[:, part]], 1)
    block = 256
    blocks = length // block
    outs = []

    def project(seq, piece):
        lanes = pl.ds(pl.multiple_of(piece * width, width), width)
        for i in range(blocks):
            rows = pl.ds(i * block, block)
            value = contract(x_all[seq, rows], w[piece], (1, 0)) + biases[piece, 0:1]
            for j in range(3):
                qkv[j, seq, rows, lanes] = value[:, j * width : (j + 1) * width].astype(BF16)

    lse[...] = jnp.zeros_like(lse)
    of_piece = heads // 3
    units = seqs * heads

    def fetch_mask(unit):
        slot = unit % 2
        return pltpu.make_async_copy(mask.at[unit % heads], masks.at[slot], mask_sem.at[slot])

    def one_head(unit, carry):
        seq, head = unit // heads, unit % heads
        relays_in_loop(unit, 0, 3, units)
        for piece in range(3):

            @pl.when(unit == piece * of_piece)
            def _():
                for index in range(2 * n_z):
                    lay_out(index, piece).wait()

        @pl.when(unit == heads)
        def _():
            exchanged(x_all, 0, 1)

        @pl.when(unit % of_piece == 0)
        def _():
            project(seq, head // of_piece)

        fetch_mask(unit).wait()

        attend_head(head, seq, qkv, masks.at[unit % 2], att, lse)

        @pl.when(unit + 2 < units)
        def _():
            fetch_mask(unit + 2).start()

        return carry

    lax.fori_loop(0, units, one_head, 0)
    outs.append(pltpu.make_async_copy(x_all, x_out, out_sem.at[0]))
    outs.append(pltpu.make_async_copy(qkv.at[pl.ds(0, 3)], qkv_out, out_sem.at[1]))
    outs.append(pltpu.make_async_copy(att, att_out, out_sem.at[2]))
    outs.append(pltpu.make_async_copy(lse, lse_out, out_sem.at[3]))
    for copy in outs:
        copy.start()
    relays(BEFORE_UP)

    def plane_from_core(x_at):
        for step in range(at.ring):
            wait(at.share(x_at, 1 - at.core, step), all_of)

    plane_from_core(at.core)
    loads = {"out": [], "down": []}
    for number, (name, share_at, first, begin, size) in enumerate(plan):
        if name != "up":
            target = {"out": w_out, "down": w_down}[name]
            source = mats.at[share_at, pl.ds(first // depth, size // depth)]
            loads[name].append(pltpu.make_async_copy(source, target.at[pl.ds(begin // depth, size // depth)], load_sem.at[number]))
    for copy in loads["out"]:
        copy.start()
    ups = [entry for entry in plan if entry[0] == "up"]
    pairs, group, filled = [], [], 0
    for _, share_at, first, _, size in ups:
        group.append((share_at, first, size))
        filled += size
        if filled // n_up % 16 == 0:
            pairs.append(group)
            group, filled = [], 0

    def fetch(number):
        slot = number % 2
        return [
            pltpu.make_async_copy(
                mats.at[share_at, pl.ds(first // depth, size // depth)],
                stage.at[slot, i, pl.ds(0, size // depth)],
                stage_sem.at[slot, i],
            )
            for i, (share_at, first, size) in enumerate(pairs[number])
        ]

    outs[1].wait()
    for copy in fetch(0):
        copy.start()
    line = 0
    for number, members in enumerate(pairs):
        if number + 1 < len(pairs):
            for copy in fetch(number + 1):
                copy.start()
        for copy in fetch(number):
            copy.wait()
        lines = sum(size for _, _, size in members) // n_up
        for j in range(n_up):
            pieces = []
            for i, (_, _, size) in enumerate(members):
                each = size // n_up
                low, high = j * each // 16 * 16, -(-(j + 1) * each // 16) * 16
                values = stage[number % 2, i].reshape(3 * depth, D)[low:high].astype(F32)
                pieces.append(values[j * each - low : j * each - low + each])
            w_up[j, line : line + lines] = jnp.concatenate(pieces, 0).astype(BF16)
        line += lines
    for copy in loads["out"]:
        copy.wait()

    b_o, b_2, g_1, s_1, g_2, s_2 = (row_of(grid, starts[i], per) for i in (2, 4, 5, 6, 7, 8))
    n_chunks = seqs * blocks

    def columns(i):
        return pl.ds(pl.multiple_of(i * block, block), block)

    def up_chunk(i, carry):
        relays_in_loop(i, BEFORE_UP + 1, n_up, n_chunks)
        seq, rows = i // blocks, columns(i % blocks)
        mixed = contract(att[seq, rows], w_out[...].reshape(D, D), (1, 0))
        n1, scale1 = norm_parts(x_all[seq, rows].astype(F32) + mixed + b_o)
        wide[seq, rows] = n1
        scales[seq, rows] = jnp.broadcast_to(scale1, (block, 128))
        h1_low = (n1 * g_1 + s_1).astype(BF16)
        h1_t[:, columns(i)] = h1_low.T
        for j in range(n_up):
            value = contract(h1_low, w_up[j], (1, 0)) + row_of(grid, starts[3] + j * per, per)
            phi = 0.5 * (1.0 + lax.erf(value * ROOT_HALF))
            act[j, seq, rows] = (value * phi).astype(BF16)
            slope[j, seq, rows] = (phi + value * (jnp.exp(-0.5 * value * value) * ROOT_TWO_PI_INV)).astype(BF16)
        return carry

    lax.fori_loop(0, n_chunks, up_chunk, 0)
    outs.append(pltpu.make_async_copy(h1_t, h1_out, out_sem.at[4]))
    outs[4].start()
    relays(LAST_STEP)

    sends.under(is_core0, functools.partial(plane_from_core, 1))
    for copy in loads["down"]:
        copy.start()
    for seq in range(seqs):
        exchanged(dy, 1, seq)
    own[2].wait()
    sums[...] = jnp.zeros_like(sums)
    for copy in loads["down"]:
        copy.wait()

    def rows_out(i):
        seq, rows = i // blocks, columns(i % blocks)
        pairs_of = (
            (wide.at[seq, rows], dr1_out.at[seq, rows]),
            (datt.at[seq, rows], datt_out.at[seq, rows]),
            (act_t.at[:, columns(i)], act_out.at[:, columns(i)]),
            (slope.at[:, seq, rows], du_out.at[:, seq, rows]),
            (dz.at[seq, rows], dz_out.at[seq, rows]),
            (da.at[seq, rows], da_out.at[seq, rows]),
        )
        return [pltpu.make_async_copy(src, dst, row_sem.at[k, i]) for k, (src, dst) in enumerate(pairs_of)]

    holders = block // tokens

    def give(i, e):
        seq = i // blocks
        holder = i % blocks * holders + e
        src = out.at[seq, pl.ds(pl.multiple_of(holder * tokens, tokens), tokens)]
        dst = out_own.at[at.seq * seqs + seq]
        step = (holder - at.seq + 4) % 4
        remote = pltpu.make_async_remote_copy(
            src_ref=src,
            dst_ref=dst,
            send_sem=give_sem.at[0, i, e],
            recv_sem=give_sem.at[1, seq, step],
            device_id={"seq": holder},
            device_id_type=MESH,
        )
        return holder != at.seq, remote, pltpu.make_async_copy(src, dst, give_own.at[seq])

    def down_chunk(i, carry):
        seq, rows = i // blocks, columns(i % blocks)
        n1 = wide[seq, rows]
        scale1 = scales[seq, rows][:, 0:1]
        total = n1 * g_1 + s_1 + b_2
        for j in range(n_up):
            value = act[j, seq, rows]
            act_t[pl.ds(j * D, D), columns(i)] = value.T
            total = total + contract(value, w_down[pl.ds(j * D // depth, D // depth)].reshape(D, D), (1, 0))
        n2, scale2 = norm_parts(total)
        out[seq, rows] = (n2 * g_2 + s_2).astype(BF16)
        for e in range(holders):
            away, remote, here = give(i, e)
            pl.when(away)(remote.start)
            pl.when(jnp.logical_not(away))(here.start)
        d = dy[seq, rows].astype(F32)
        sums[0:1] += jnp.sum(d * n2, 0, keepdims=True)
        sums[1:2] += jnp.sum(d, 0, keepdims=True)
        dr2 = norm_back(d, n2, scale2, g_2)
        dz_low = dr2.astype(BF16)
        dz[seq, rows] = dz_low
        dh1 = dr2
        for j in range(n_up):
            grad = contract(dz_low, w_down[pl.ds(j * D // depth, D // depth)].reshape(D, D), (1, 1))
            du = (grad * slope[j, seq, rows].astype(F32)).astype(BF16)
            slope[j, seq, rows] = du
            dh1 = dh1 + contract(du, w_up[j], (1, 1))
        sums[2:3] += jnp.sum(dh1 * n1, 0, keepdims=True)
        sums[3:4] += jnp.sum(dh1, 0, keepdims=True)
        d1 = norm_back(dh1, n1, scale1, g_1)
        wide[seq, rows] = d1
        da_low = d1.astype(BF16)
        da[seq, rows] = da_low
        datt[seq, rows] = contract(da_low, w_out[...].reshape(D, D), (1, 1)).astype(BF16)
        for copy in rows_out(i):
            copy.start()
        return carry

    lax.fori_loop(0, n_chunks, down_chunk, 0)

    for i in range(n_chunks):
        for copy in rows_out(i):
            copy.wait()
        for e in range(holders):
            away, remote, here = give(i, e)
            pl.when(away)(remote.wait_send)
            pl.when(jnp.logical_not(away))(here.wait)
    for seq in range(seqs):
        for step in (1, 2, 3):
            dst = out_own.at[at.seq_at(4 - step) * seqs + seq]
            sends.arrived(dst, give_sem.at[1, seq, step], at.core_peer)
    for copy in outs[:1] + outs[2:]:
        copy.wait()
    sends.drain(at.core_peer)


def forward(n_batch, flat, vec, x_in, grad_in, scored, mask):
    rows = flat.shape[0] * 128 // D
    depth = rows // 3
    shares = 4 * n_batch
    n_z = n_batch // 2
    n_up = FF // D
    seqs, length = x_in.shape[0] // 4, 4 * x_in.shape[1]
    tokens = seqs * length
    plan = []
    for number in range(shares):
        for name, _, at, begin, size in segments(number, rows):
            if name != "qkv":
                plan.append((name, number, at, begin, size))
    whole, low, gelu = (seqs, length, D), (D, tokens), (n_up, seqs, length, D)
    outs = [
        ((shares, 3, depth, D), BF16),
        (whole, BF16),
        ((3,) + whole, BF16),
        (whole, BF16),
        ((seqs, length, 128), F32),
        (x_in.shape, BF16),
        (whole, F32),
        (whole, BF16),
        ((FF, tokens), BF16),
        (gelu, BF16),
        (low, BF16),
        (whole, BF16),
        (whole, BF16),
        ((8, D), F32),
    ]
    vmem = [
        (whole, BF16),
        (whole, BF16),
        (whole, BF16),
        (x_in.shape, BF16),
        (whole, BF16),
        ((rows, D), F32),
        ((3, depth, D), BF16),
        (whole, F32),
        (whole, BF16),
        ((D // depth, depth, D), BF16),
        ((n_up, D, D), BF16),
        ((FF // depth, depth, D), BF16),
        ((2, 2, 3, depth, D), BF16),
        (gelu, BF16),
        ((FF, tokens), BF16),
        (gelu, BF16),
        (low, BF16),
        (whole, BF16),
        (whole, BF16),
        ((seqs, length, 128), F32),
        ((3, 8, D), F32),
        ((seqs, length, 128), F32),
        ((2, length, length), jnp.int32),
        (vec.shape, F32),
        ((3 * n_z + 3,) + vec.shape, F32),
    ]
    blocks = tokens // 256
    sems = [(3,), (400,), (shares, 3), (n_z + 3,), (2, seqs, 4), (2 * n_z, 3), (2,), (5,), (len(plan),), (2, 2), (6, blocks), (2, blocks, 4), (seqs,), (x_in.shape[0],)]
    return pl.pallas_call(
        functools.partial(forward_kernel, n_batch, plan),
        out_shape=[jax.ShapeDtypeStruct(shape, dtype) for shape, dtype in outs],
        in_specs=[VMEM, VMEM, ANY, ANY, VMEM, ANY],
        out_specs=[ANY] * 13 + [VMEM],
        scratch_shapes=[pltpu.VMEM(shape, dtype) for shape, dtype in vmem]
        + [pltpu.SemaphoreType.DMA(shape) for shape in sems],
        compiler_params=pltpu.CompilerParams(
            collective_id=0, has_side_effects=True, vmem_limit_bytes=60 * MIB
        ),
        name="forward",
    )(flat, vec, x_in, grad_in, scored, mask)


PLACES = (4, 3, -3, 2, -2, 1, -1, 0)
REDUCE_TIMES = {
    0: dict(over_x=(-2, 0, -2, 13, 6, 21, 16, 6), late=((6, 15, 16, 22, 26, 28), (20, 23, 27, 28, 28, 28), (6, 26, 27, 27, 28, 28))),
    1: dict(kind0=(11, 18, 25, 28, 28), kind1=(-2, -1, 5, 8, 14, 22)),
    2: dict(kind0=(6, 12, 21, 27, 28), late=((3, 11, 21, 25, 27, 27), (3, 20, 23, 25, 28, 28), (4, 26, 27, 27, 28, 28))),
    3: dict(over_x=(4, 7, 13, 17, 6, 20, 6, 21), kind1=(-2, 1, 11, 17, 28, 28)),
}


def reduction_table():
    found = []
    ring = (("begin",), ("hop", 1), ("hop", 2), ("hop", 3), ("end",), ("last",))
    for seq, times in REDUCE_TIMES.items():
        for i, step in enumerate(times.get("over_x", ())):
            found.append((step, 0, i, seq, ("x", PLACES[i])))
        for kind in (0, 1):
            for i, step in enumerate(times.get(f"kind{kind}", ())):
                found.append((step, 1 + kind, i, seq, ("ring", kind, None) + ring[i]))
        for piece in range(3):
            for i, step in enumerate(times.get("late", ((), (), ()))[piece]):
                found.append((max(step, 8 * (piece + 1)), 3 + piece, i, seq, ("ring", 1, piece) + ring[i]))
    table = {}
    for step, _, _, seq, what in sorted(found):
        table.setdefault((seq, step), []).append(what)
    return table


def finish_kernel(
    n_batch, mask, qkv_in, att_in, datt_in, lse_in, x_in, mats, dr1_in, act_in, du_in, h1_in, dz_in, da_in, sums,
    share, vec_out, dx_own,
    qkv, att, datt, lse, w, wide, dqkv, dx, act_t, masks, probs, dscore, grads, from_core, x_a, ring_in, x_b, total, vec_in,
    in_sem, mask_sem, act_sem, du_sem, own_sem, send_sem, core_sem, a_sem, ring_sem, b_sem, vec_sem, seq_sem,
):
    at = Place(n_batch)
    rows = grads.shape[2]
    heads = mask.shape[0]
    n_z, tokens = at.n_z, dx_own.shape[1]
    seqs, length = att.shape[:2]
    depth = rows // 3
    n_up = FF // D
    half = at.ring // 2
    sends = Sends(send_sem)
    mine = pl.ds(at.seq * tokens, tokens)
    dz, da, x = dqkv.at[2], dx, dx
    turned, h1_t = act_t.at[0], act_t.at[1]

    ins = [
        pltpu.make_async_copy(src, dst, in_sem.at[i])
        for i, (src, dst) in enumerate(
            ((dz_in, dz), (att_in, att), (da_in, da), (qkv_in, qkv), (datt_in, datt), (lse_in, lse))
        )
    ]

    def fetch_act(j):
        return pltpu.make_async_copy(act_in.at[pl.ds(j * D, D)], act_t.at[j % 2], act_sem.at[j % 2])

    def fetch_du(j):
        return pltpu.make_async_copy(du_in.at[j], dqkv.at[j % 2], du_sem.at[j % 2])

    def fetch_mask(head):
        slot = head % 2
        return pltpu.make_async_copy(mask.at[head], masks.at[slot], mask_sem.at[slot])

    ins[0].start()
    down_order = [*range(1, n_up), 0]
    fetch_act(down_order[0]).start()
    fetch_act(down_order[1]).start()
    for copy in ins[1:]:
        copy.start()
    fetch_du(0).start()
    fetch_du(1).start()
    fetch_mask(0).start()
    fetch_mask(1).start()
    loads = []
    for index in range(n_batch):
        target = w.at[:, pl.ds(index * depth, depth)]
        loads.append(pltpu.make_async_copy(mats.at[index], target, in_sem.at[9 + index]))
        loads[-1].start()
    at.barrier()

    is_class = [at.seq == seq for seq in range(4)]
    on_core = (at.core == 0, at.core == 1)

    def plane_of(core, kind):
        return (2 - core, 3 * core)[kind]

    order = [half] + [sign * hops for hops in range(half - 1, 0, -1) for sign in (1, -1)] + [0]

    def part_rows(part):
        return pl.ds(part[0] * depth, (part[1] - part[0]) * depth)

    def to_core(core, kind, part=(0, 3)):
        lines = part_rows(part)
        for step in order:
            b = at.around(step)
            source = grads.at[plane_of(1 - core, kind), b, lines]
            sends.start(source, from_core.at[kind, b, lines], core_sem.at[kind, b, part[0]], at.core_peer, lambda: from_core.at[0, 0, lines])

    def is_own(seq, kind):
        return (seq // 2 == seq % 2) == (kind == 1)

    def ring_of(own, kind, piece):
        if piece is not None:
            part = (piece, piece + 1)
            return part, (part, None) if piece == 0 else (None, part)
        if kind == 1 or own:
            return (0, 3), ((0, 1), (1, 3))
        return None, (None, None)

    def add(seq, kind, b, part, *others, into=None):
        low, high = part
        terms = [grads.at[plane_of(seq % 2, kind), b], *others]
        if kind == 0 and is_own(seq, 0):
            terms.append(x_a.at[b])
        lines = part_rows(part)
        target = from_core.at[kind, b]
        if into is not None:
            into[lines] = from_core[kind, b, lines].astype(F32)
            target = into
        add_rows(target, (low * depth, (high - low) * depth), *[(ref, low * depth) for ref in terms])

    def ready(seq, kind, b, piece):
        part = (0, 3) if piece is None else (piece, piece + 1)
        here = from_core.at[kind, b, part_rows(part)]
        if not (kind == 0 and not is_own(seq, 0)):
            sends.arrived(here, core_sem.at[kind, b, part[0]], at.core_peer)
        if kind == 0 and is_own(seq, 0):
            sends.arrived(x_a.at[b], a_sem.at[b], at.core_peer)

    def slot(way, hops):
        return 1 + way * (half - 1) + hops - 1 if hops else 0

    def ring_send(kind, b, way, hops, part):
        peer = (at.next, at.prev)[way]
        lines = part_rows(part)
        sends.start(from_core.at[kind, b, lines], ring_in.at[kind, slot(way, hops), lines], ring_sem.at[kind, way, hops, part[0]], peer, lambda: ring_in.at[0, 0, lines])

    def ring_wait(kind, way, hops, part):
        here = ring_in.at[kind, slot(way, hops)]
        sends.arrived(here.at[part_rows(part)], ring_sem.at[kind, way, hops, part[0]], at.core_peer)
        return here

    def ring_step(seq, kind, piece, what, hops=0):
        own = is_own(seq, kind)
        whole, opposite = ring_of(own, kind, piece)
        if what == "begin":
            b = at.around(half)
            ready(seq, kind, b, piece)
            for way, part in enumerate(opposite):
                if part:
                    add(seq, kind, b, part)
                    ring_send(kind, b, way, 0, part)
        elif what == "hop":
            for way, b in enumerate((at.around(half - hops), at.around(hops - half))):
                ready(seq, kind, b, piece)
                if hops > 1:
                    add(seq, kind, b, whole, ring_wait(kind, way, hops - 1, whole))
                else:
                    part = opposite[way]
                    if part:
                        add(seq, kind, b, part, ring_wait(kind, way, 0, part))
                    for low, high in ((whole[0], part[0]), (part[1], whole[1])) if part else (whole,):
                        if low < high:
                            add(seq, kind, b, (low, high))
                ring_send(kind, b, way, hops, whole)
        elif what == "end":
            b = at.batch
            ready(seq, kind, b, piece)
            others = [ring_wait(kind, way, half - 1, whole) for way in range(2)]
            add(seq, kind, b, whole, *others, into=total if own else None)
            if not own:
                lines = part_rows(whole)
                sends.start(from_core.at[kind, b, lines], x_b.at[lines], b_sem.at[whole[0]], at.x_peer, lambda: x_b.at[lines])
        elif own:
            far_part = ring_of(False, kind, piece)[0]
            sends.arrived(x_b.at[part_rows(far_part)], b_sem.at[far_part[0]], at.core_peer)
            add_rows(total, (far_part[0] * depth, (far_part[1] - far_part[0]) * depth), (x_b, far_part[0] * depth))

    def over_x(seq, step):
        b = at.around(step)
        here = from_core.at[0, b]
        sends.arrived(here, core_sem.at[0, b, 0], at.core_peer)
        add(seq, 0, b, (0, 3))
        sends.start(here, x_a.at[b], a_sem.at[b], at.x_peer, lambda: x_a.at[0])

    table = reduction_table()

    def reduce_at(step):
        for seq in range(4):
            some = table.get((seq, step))
            if some:
                steps = [functools.partial(over_x if what[0] == "x" else ring_step, seq, *what[1:]) for what in some]
                sends.under(is_class[seq], functools.partial(run, steps))

    base_down, base_up, base_out = 3 * D + D + FF, 3 * D + D, 3 * D

    def put(row, values):
        done = 0
        while done < values.shape[0]:
            number, first = (row + done) // rows, (row + done) % rows
            size = min(values.shape[0] - done, rows - first)
            grads[number // n_batch, number % n_batch, first : first + size] = values[done : done + size]
            done += size

    starts, offset = [], 0
    for size in VEC_LENGTHS:
        starts.append(offset // 128)
        offset += size
    per = D // 128

    def put_vec(first, value):
        for i in range(value.shape[1] // 128):
            vec_out[first + i : first + i + 1, :] = value[0:1, i * 128 : (i + 1) * 128]

    ones = jnp.ones((16, seqs * length), BF16)
    block = D // 2

    def flat(values):
        return values.reshape(seqs * length, D)

    vec_out[...] = jnp.zeros_like(vec_out)
    ins[0].wait()
    for number, j in enumerate(down_order):
        fetch_act(j).wait()
        for i in range(D // block):
            put(base_down + j * D + i * block, contract(act_t[j % 2, i * block : (i + 1) * block], flat(dz[...]), (1, 0)).astype(BF16))
        if number + 2 < n_up:
            fetch_act(down_order[number + 2]).start()
        if number == n_up - 2:
            sends.under(on_core[0], functools.partial(to_core, 0, 1))
            h1_copy = pltpu.make_async_copy(h1_in, h1_t, in_sem.at[9 + n_batch])
            h1_copy.start()
    put_vec(starts[4], contract(ones, flat(dz[...]), (1, 0)))
    reduce_at(-3)
    h1_copy.wait()
    ups = []
    for number in range(4 * n_batch):
        ups += [(number, at_row, begin, size) for name, _, at_row, begin, size in segments(number, rows) if name == "up"]
    middle = D // 2
    for high in (1, 0):
        for pair in range(n_up // 2):
            for k in range(2):
                j = pair * 2 + k
                fetch_du(j).wait()
                wide[k, 0:middle] = contract(h1_t[high * middle : (high + 1) * middle], flat(dqkv[j % 2]), (1, 0))
                if high:
                    put_vec(starts[3] + j * per, contract(ones, flat(dqkv[j % 2]), (1, 0)))
                if not (high == 0 and pair == n_up // 2 - 1):
                    fetch_du((j + 2) % n_up).start()
            for number, at_row, begin, size in ups:
                count, low = size // n_up, begin // n_up - high * middle
                if 0 <= low < middle:
                    both = jnp.concatenate([wide[k, low : low + count] for k in range(2)], 0).astype(BF16)
                    at_row += pair * 2 * count
                    grads[number // n_batch, number % n_batch, at_row : at_row + 2 * count] = both
        if high:
            sends.under(on_core[1], functools.partial(to_core, 1, 0))
            reduce_at(-2)
    ins[1].wait()
    ins[2].wait()
    for seq in range(seqs):
        turned[:, seq * length : (seq + 1) * length] = att[seq].T
    for i in range(D // block):
        put(base_out + i * block, contract(turned[i * block : (i + 1) * block], flat(da[...]), (1, 0)).astype(BF16))
    sends.under(on_core[0], functools.partial(to_core, 0, 0))
    put_vec(starts[2], contract(ones, flat(da[...]), (1, 0)))
    for i, line in enumerate((starts[7], starts[8], starts[5], starts[6])):
        put_vec(line, sums[i : i + 1])

    dr1_copy = pltpu.make_async_copy(dr1_in, wide, in_sem.at[8])
    dr1_copy.start()
    x_copy = pltpu.make_async_copy(x_in, x, in_sem.at[7])
    x_copy.start()
    for copy in ins[3:]:
        copy.wait()
    x_copy.wait()
    for seq in range(seqs):
        turned[:, seq * length : (seq + 1) * length] = x[seq].T

    reduce_at(-1)

    units = heads * seqs
    of_piece = heads // 3
    width = D // 3
    lines = 4 * depth

    def qkv_gradient(piece):
        lanes = slice(piece * width, (piece + 1) * width)
        for j in range(3):
            right = dqkv[j, :, :, lanes].reshape(seqs * length, width)
            for i in range(D // lines):
                values = contract(turned[i * lines : (i + 1) * lines], right, (1, 0)).astype(BF16)
                for k in range(4):
                    grads[0, 4 * i + k, piece * depth : (piece + 1) * depth, j * width : (j + 1) * width] = values[k * depth : (k + 1) * depth]
        sends.under(on_core[1], functools.partial(to_core, 1, 1, (piece, piece + 1)))

    def one_head(head, carry):
        fetch_mask(head).wait()

        def one_seq(seq, carry):
            dispatch(head * seqs + seq, [step for step in range(units) if any((some, step) in table for some in range(4))], reduce_at)
            head_backward(head, seq, qkv, masks.at[head % 2], att, datt, lse, probs, dscore, dqkv)
            return carry

        lax.fori_loop(0, seqs, one_seq, 0)

        @pl.when(head + 2 < heads)
        def _():
            fetch_mask(head + 2).start()

        for piece in range(3):
            pl.when(head == (piece + 1) * of_piece - 1)(functools.partial(qkv_gradient, piece))
        return carry

    lax.fori_loop(0, heads, one_head, 0)
    for j in (0, 2):
        put_vec(starts[j // 2], contract(ones, flat(dqkv[j]), (1, 0)))

    def vec_hop(hop, peer):
        vec_in[hop + n_z] = vec_out[...]
        sends.start(vec_in.at[hop + n_z], vec_in.at[hop], vec_sem.at[hop], peer)

    def vec_take(hop):
        sends.arrived(vec_in.at[hop], vec_sem.at[hop], at.core_peer)
        vec_out[...] = vec_out[...] + vec_in[hop]

    vec_hop(0, at.core_peer)

    dr1_copy.wait()
    for copy in loads:
        copy.wait()
    for number, step in enumerate((1, 2, 3, 0)):
        reduce_at(units + number)
        theirs = pl.ds(pl.multiple_of(at.seq_at(step) * tokens, tokens), tokens)
        for seq in range(seqs):
            value = wide[seq, theirs]
            for j in range(3):
                for piece in range(3):
                    left = dqkv[j, seq, theirs, piece * width : (piece + 1) * width]
                    value = value + contract(left, w[piece, :, j * width : (j + 1) * width], (1, 1))
            dx[seq, theirs] = value.astype(BF16)
        there = dx_own.at[pl.ds(at.seq * seqs, seqs)]
        if step:
            sends.start(dx.at[:, theirs], there, seq_sem.at[step], at.seq_peer(step), lambda: dx.at[:, pl.ds(0, tokens)])
        if number == 1:
            vec_take(0)
            vec_hop(1, at.x_peer)
    own_dx = pltpu.make_async_copy(dx.at[:, mine], dx_own.at[pl.ds(at.seq * seqs, seqs)], own_sem.at[0])
    own_dx.start()
    vec_take(1)
    vec_hop(2, at.y_peer)
    reduce_at(units + 4)
    vec_take(2)
    vec_in[2 * n_z + 2] = vec_out[...]
    for step in range(1, n_z):
        sends.start(vec_in.at[2 * n_z + 2], vec_in.at[2 + 2 * n_z + step], vec_sem.at[3 + step], at.z_peer(step))
    reduce_at(units + 5)

    def in_flat_order(layout):
        for flat_rows, lines, lanes in share_blocks(layout):
            share[flat_rows, :] = total[lines, lanes]

    for_share(at.seq * n_batch + at.batch, 4 * n_batch, rows, in_flat_order)
    for step in range(1, n_z):
        slot_in = 2 + 2 * n_z + step
        sends.arrived(vec_in.at[slot_in], vec_sem.at[3 + step], at.core_peer)
        vec_out[...] = vec_out[...] + vec_in[slot_in]
    for step in (1, 2, 3):
        theirs = pl.ds(at.seq_at(4 - step) * seqs, seqs)
        sends.arrived(dx_own.at[theirs], seq_sem.at[step], at.core_peer)
    own_dx.wait()
    sends.drain(at.core_peer)


def finish(n_batch, mask, qkv, att, datt, lse, x, mats, dr1, act_t, du, h1_t, dz, da, sums):
    _, _, depth, _ = mats.shape
    rows = 3 * depth
    length = mask.shape[1]
    n_z = n_batch // 2
    seqs = att.shape[0]
    whole = (att.shape, BF16)
    vec = (sum(VEC_LENGTHS) // 128, 128)
    vmem = [
        (qkv.shape, BF16),
        whole,
        whole,
        (lse.shape, F32),
        ((3, D, D), BF16),
        (att.shape, F32),
        (qkv.shape, BF16),
        whole,
        ((2, D, seqs * length), BF16),
        ((2, length, length), jnp.int32),
        ((length, length), BF16),
        ((length, length), BF16),
        ((4, n_batch, rows, D), BF16),
        ((2, n_batch, rows, D), BF16),
        ((n_batch, rows, D), BF16),
        ((2, 2 * n_z - 1, rows, D), BF16),
        ((rows, D), BF16),
        ((rows, D), F32),
        ((3 * n_z + 3,) + vec, F32),
    ]
    sems = [(10 + n_batch,), (2,), (2,), (2,), (1,), (400,), (2, n_batch, 3), (n_batch,), (2, 2, n_z, 3), (3,), (n_z + 3,), (4,)]
    return pl.pallas_call(
        functools.partial(finish_kernel, n_batch),
        out_shape=(
            jax.ShapeDtypeStruct((rows * D // 128, 128), F32),
            jax.ShapeDtypeStruct(vec, F32),
            jax.ShapeDtypeStruct((seqs * 4, length // 4, D), BF16),
        ),
        in_specs=[ANY] * 13 + [VMEM],
        out_specs=[VMEM, VMEM, ANY],
        scratch_shapes=[pltpu.VMEM(shape, dtype) for shape, dtype in vmem]
        + [pltpu.SemaphoreType.DMA(shape) for shape in sems],
        compiler_params=pltpu.CompilerParams(
            collective_id=1, has_side_effects=True, vmem_limit_bytes=62 * MIB
        ),
        name="finish",
    )(mask, qkv, att, datt, lse, x, mats, dr1, act_t, du, h1_t, dz, da, sums)


def attention(qkv, mask):
    heads = mask.shape[0]
    q, k, v = (part.reshape(part.shape[:2] + (heads, D // heads)) for part in qkv)
    scores = jnp.einsum("bqhd,bkhd->bhqk", q, k, preferred_element_type=F32) / math.sqrt(D // heads)
    scores = jnp.where(mask > 0, scores, NEG_FILL)
    largest = jnp.max(scores, -1, keepdims=True)
    expo = jnp.exp(scores - largest)
    total = jnp.sum(expo, -1, keepdims=True)
    probs = (expo / total).astype(BF16)
    mixed = jnp.einsum("bhqk,bkhd->bqhd", probs, v, preferred_element_type=F32)
    return mixed.astype(BF16).reshape(qkv.shape[1:])


def middle_plain(mats, vecs, x, att, dy):
    pieces, offset = [], 0
    for size in VEC_LENGTHS:
        pieces.append(vecs.reshape(-1)[offset : offset + size])
        offset += size
    _, _, b_o, b_1, b_2, g_1, s_1, g_2, s_2 = pieces
    w_out, w_down = (take_matrix(mats, name)[0] for name in ("out", "down"))
    w_up = take_matrix(mats, "up").swapaxes(0, 1).reshape(D, FF)
    r1 = x.astype(F32) + jnp.dot(att, w_out, preferred_element_type=F32) + b_o
    h1 = layer_norm(r1, g_1, s_1)
    h1_low = h1.astype(BF16)
    up = jnp.dot(h1_low, w_up, preferred_element_type=F32) + b_1
    act = gelu_exact(up).astype(BF16)
    r2 = h1 + jnp.dot(act, w_down, preferred_element_type=F32) + b_2
    out = layer_norm(r2, g_2, s_2).astype(BF16)
    _, norm_two_back = jax.vjp(layer_norm, r2, g_2, s_2)
    dr2, dg_2, ds_2 = norm_two_back(dy.astype(F32))
    dz = dr2.astype(BF16)
    _, gelu_back = jax.vjp(gelu_exact, up)
    du = gelu_back(contract_cols(dz, w_down))[0].astype(BF16)
    dh1 = dr2 + contract_cols(du, w_up)
    _, norm_one_back = jax.vjp(layer_norm, r1, g_1, s_1)
    dr1, dg_1, ds_1 = norm_one_back(dh1)
    da = dr1.astype(BF16)
    datt = contract_cols(da, w_out).astype(BF16)
    mats_grad = {
        "out": contract_rows(att, da)[None],
        "up": contract_rows(h1_low, du).reshape(D, FF // D, D).swapaxes(0, 1),
        "down": contract_rows(act, dz)[None],
    }
    sums = [jnp.sum(member.astype(F32), 0) for member in (da, du, dz)]
    return out, dr1, datt, mats_grad, jnp.concatenate(sums + [dg_1, ds_1, dg_2, ds_2])


def finish_plain(mask, qkv, datt, x, w_qkv, dr1):
    heads = mask.shape[0]
    seqs, length, _ = x.shape
    split = (seqs, length, heads, D // heads)
    q, k, v = (part.reshape(split) for part in qkv)
    g = datt.reshape(split)
    scale = 1.0 / math.sqrt(D // heads)
    scores = jnp.einsum("bqhd,bkhd->bhqk", q, k, preferred_element_type=F32) * scale
    probs = jax.nn.softmax(jnp.where(mask > 0, scores, NEG_FILL), -1)
    dprobs = jnp.einsum("bqhd,bkhd->bhqk", g, v, preferred_element_type=F32)
    inner = jnp.sum(probs * dprobs, -1, keepdims=True)
    dscore = (probs * (dprobs - inner)).astype(BF16)
    dq = jnp.einsum("bhqk,bkhd->bqhd", dscore, k, preferred_element_type=F32) * scale
    dk = jnp.einsum("bhqk,bqhd->bkhd", dscore, q, preferred_element_type=F32) * scale
    dv = jnp.einsum("bhqk,bqhd->bkhd", probs.astype(BF16), g, preferred_element_type=F32)
    dqkv = jnp.stack([dq, dk, dv]).astype(BF16).reshape(3, seqs * length, D)
    dw = jnp.stack([contract_rows(x.reshape(-1, D), part) for part in dqkv])
    dx = dr1 + sum(contract_cols(dqkv[j], w_qkv[j]) for j in range(3))
    db = [jnp.sum(dqkv[j].astype(F32), 0) for j in (0, 2)]
    return dw, dx.astype(BF16).reshape(x.shape), jnp.concatenate(db)


def local(
    n_batch,
    inputs,
    out_grad,
    out_mask,
    attn_mask,
    mat_param,
    mat_first,
    mat_second,
    vec_param,
    vec_first,
    vec_second,
):
    shares = 4 * n_batch
    share_rows = mat_param.shape[0] // D
    vec_len = vec_param.shape[0]
    me = lax.axis_index("seq") * n_batch + lax.axis_index("batch")

    vec_share = lax.dynamic_update_slice(
        jnp.zeros((shares * vec_len,), F32), vec_param.astype(BF16).astype(F32), (me * vec_len,)
    ).reshape(-1, 128)
    if share_rows % 96 == 0 and share_rows * n_batch == 3 * D:
        mats, x_all, qkv, attended, lse, outputs, *middle = forward(
            n_batch, mat_param.reshape(-1, 128), vec_share, inputs, out_grad, out_mask, attn_mask
        )
        dr1, datt, *middle = middle
        mat_grad, vec_sum, dx = finish(n_batch, attn_mask, qkv, attended, datt, lse, x_all, mats, dr1, *middle)
        mat_grad = mat_grad.reshape(-1)
        vec_grad = lax.dynamic_slice_in_dim(vec_sum.reshape(-1), me * vec_len, vec_len)
    else:
        share = rearrange(me, shares, mat_param.reshape(share_rows, D).astype(BF16), by_columns)
        mats = lax.all_gather(share, ("seq", "batch"))
        vecs = lax.psum(vec_share, ("seq", "batch")).reshape(-1)
        dy_low = (out_grad * out_mask[..., None].astype(F32)).astype(BF16)
        x_all, dy_all = (
            lax.all_to_all(member, "seq", 0, 1, tiled=True) for member in (inputs, dy_low)
        )
        whole = x_all.shape
        flat = (whole[0] * whole[1], D)
        w_qkv = regroup(take_matrix(mats, "qkv"))
        proj = jnp.stack([jnp.dot(x_all.reshape(flat), part, preferred_element_type=F32) for part in w_qkv])
        proj = proj + jnp.stack([vecs[:D], jnp.zeros((D,), F32), vecs[D : 2 * D]])[:, None]
        qkv = proj.astype(BF16).reshape((3,) + whole)
        attended = attention(qkv, attn_mask).reshape(flat)
        out_all, dr1, datt, mats_grad, grad_vecs = middle_plain(
            mats, vecs, x_all.reshape(flat), attended, dy_all.reshape(flat)
        )
        mats_grad["qkv"], dx_all, db = finish_plain(attn_mask, qkv, datt, x_all, w_qkv, dr1)
        mats_grad["qkv"] = regroup(mats_grad["qkv"])
        grads = to_shares({name: part.astype(BF16) for name, part in mats_grad.items()}, shares)
        mat_grad = lax.psum_scatter(grads.astype(F32), ("seq", "batch"))
        mat_grad = rearrange(me, shares, mat_grad, by_rows).reshape(-1)
        vec_grad = lax.psum_scatter(jnp.concatenate([db, grad_vecs]), ("seq", "batch"), tiled=True)
        outputs, dx = (
            lax.all_to_all(member, "seq", 1, 0, tiled=True) for member in (out_all.reshape(whole), dx_all)
        )
    return (
        outputs,
        dx.astype(F32),
        *adam_step(mat_param, mat_first, mat_second, mat_grad, MATS_RATE),
        *adam_step(vec_param, vec_first, vec_second, vec_grad, VECS_RATE),
    )


def solution(mesh):
    flat = P(("seq", "batch"))
    tokens = P("batch", "seq", None)
    return jax.shard_map(
        functools.partial(local, mesh.shape["batch"]),
        mesh=mesh,
        in_specs=(tokens, tokens, P("batch", "seq"), P()) + (flat,) * 6,
        out_specs=(tokens, tokens) + (flat,) * 6,
        check_vma=False,
    )
```
